32 devices in a mesh: row: 8 (over z, x), col: 4 (over y, core).
Axes of the slice: x: 2, y: 2, z: 4, core: 2. Of those that a mesh axis runs over, the one named last changes fastest.
Arguments:
- object_field: float32 [2, 2048, 1024], P(None, 'row', 'col'), may hold values from -4.2 to 4.2
- probe_modes: float32 [2, 256, 512], P(None, 'row', 'col'), may hold values from -4.2 to 4.2
- measured: float32 [8, 4, 2, 256, 256], P('row', 'col'), may hold values from 0.3 to 3
- positions: int32 [8, 4, 2, 2], P('row', 'col'), may hold values from 0 to 128
- subset_order: int32 [8, 4, 2], P('row', 'col'), may hold values from 0 to 1, each once within a row
Outputs:
- object_out: float32 [2, 2048, 1024], P(None, 'row', 'col')
- probe_out: float32 [2, 256, 512], P(None, 'row', 'col')
The draws below stay inside these ranges and needn't reach their ends.
Inputs may be any that keep to these rules, and one draw needn't show every extreme that they name: `positions`: A window of 256 pixels at these offsets lies inside the tile extended by 64 pixels on each side. `subset_order`: each tile's list is a permutation of its position numbers.
All inputs are finite; a program needn't handle non-finite values.
Results may differ from the reference program's by a relative error of at most 0.0017.
Values sent between devices are 32-bit elements; how exact they have to be, the bound alone decides.
A program may use at most 64 MiB of HBM per device.

```python
import math
import jax
import jax.numpy as jnp
from jax import lax

W = 256
MODES = 2
MARGIN = 64
TILE = 256
POS_DEV = 2
SUBSETS = 2
OUTER = 2
NR = 2048
NC = 1024
POSITIONS = 64
N_ROW = 8
N_COL = 4


def place_ends(array, key, low, top_value):
    dims = array.shape
    index_at = [jax.random.randint(jax.random.fold_in(key, axis), (), 0, dims[axis]) for axis in range(len(dims))]
    array = array.at[tuple(index_at)].set(low)
    longest = dims.index(max(dims))
    index_at[longest] = (index_at[longest] + 1) % dims[longest]
    return array.at[tuple(index_at)].set(top_value)


def shard_levels(stream_key, shape, pieces, low, high):
    loudness = 1.0
    for dim, parts in pieces:
        draws = jax.random.uniform(jax.random.fold_in(jax.random.fold_in(stream_key, 6), dim), (parts,), jnp.float32, low / len(pieces), high / len(pieces))
        loudness = loudness * jnp.repeat(jnp.exp(draws), shape[dim] // parts).reshape((-1,) + (1,) * (len(shape) - 1 - dim))
    return loudness


def normal_values(key, dims, width, limit, shards=(), kind=jnp.bfloat16):
    loudness = shard_levels(key, dims, shards, -0.22, 0.18) if shards else 1.0
    entries = jax.random.normal(key, dims, jnp.float32) * width * loudness
    return jnp.minimum(jnp.maximum(entries, -limit), limit).astype(kind)


def setup_inputs(seed: int = 0) -> dict:
    arg_keys = jax.random.split(jax.random.key(seed), 6)
    object_field = normal_values(arg_keys[0], (2, NR, NC), 0.7, 4.2, ((1, 8), (2, 4)), jnp.float32)
    probe_modes = normal_values(arg_keys[1], (MODES, W, 2 * W), 0.7, 4.2, ((1, 8), (2, 4)), jnp.float32)
    measured = jnp.clip(jnp.exp(math.log(3.0) - 2.3025851 * jax.random.uniform(arg_keys[2], (N_ROW, N_COL, POS_DEV, W, W), jnp.float32) ** shard_levels(arg_keys[2], (N_ROW, N_COL, POS_DEV, W, W), ((0, 8), (1, 4)), -0.2, 0.2)), 0.3, 3.0)
    positions = place_ends(jax.random.randint(arg_keys[3], (N_ROW, N_COL, POS_DEV, 2), 0, TILE + 2 * MARGIN - W + 1), jax.random.fold_in(arg_keys[3], 1), 0, TILE + 2 * MARGIN - W).astype(jnp.int32)
    subset_order = jax.vmap(lambda own: jax.random.permutation(own, POS_DEV))(jax.random.split(arg_keys[4], N_ROW * N_COL)).reshape((N_ROW, N_COL, POS_DEV)).astype(jnp.int32)
    return dict(object_field=object_field, probe_modes=probe_modes, measured=measured, positions=positions, subset_order=subset_order)


amp_floor = 0.3
object_rate = 0.05

def tables(probe_size):
    ramp_values = jnp.arange(probe_size, dtype=jnp.int32)
    phases = ramp_values[:, None] * ramp_values[None, :] % probe_size
    angles = phases.astype(jnp.float32) * (2.0 * math.pi / probe_size)
    norming = 1.0 / math.sqrt(probe_size)
    cosine = jnp.cos(angles) * norming
    sine_part = jnp.sin(angles) * norming
    left_tables = jnp.stack([cosine, sine_part]).astype(jnp.bfloat16)
    right_forward = jnp.concatenate([jnp.concatenate([cosine, -sine_part], 1), jnp.concatenate([sine_part, cosine], 1)], 0).astype(jnp.bfloat16)
    right_inverse = jnp.concatenate([jnp.concatenate([cosine, sine_part], 1), jnp.concatenate([-sine_part, cosine], 1)], 0).astype(jnp.bfloat16)
    return (left_tables, right_forward, right_inverse)

def halves(values):
    middle = values.shape[-1] // 2
    return (values[..., :middle], values[..., middle:])

def multiply(former, latter, conjugate):
    former_re, former_im = halves(former)
    latter_re, latter_im = halves(latter)
    if conjugate:
        return jnp.concatenate([former_re * latter_re + former_im * latter_im, former_re * latter_im - former_im * latter_re], -1)
    return jnp.concatenate([former_re * latter_re - former_im * latter_im, former_re * latter_im + former_im * latter_re], -1)

def left_apply(left_tables, stacked, direction):
    products = jnp.einsum('tij,bjk->tbik', left_tables.astype(jnp.float32), stacked.astype(jnp.float32))
    cos_re, cos_im = halves(products[0])
    sin_re, sin_im = halves(products[1])
    return jnp.concatenate([cos_re + direction * sin_im, cos_im - direction * sin_re], -1)

def project(windows, probe_full, amplitudes, left_tables, right_forward, right_inverse):
    exit_wave = multiply(probe_full[None], windows[:, None], False)
    count, mode_count, rows_here, cols_here = exit_wave.shape
    stacked = exit_wave.reshape(count * mode_count, rows_here, cols_here).astype(jnp.bfloat16)
    half_transform = left_apply(left_tables, stacked, 1.0).astype(jnp.bfloat16)
    far_field = jnp.einsum('bik,kl->bil', half_transform.astype(jnp.float32), right_forward.astype(jnp.float32))
    far_field = far_field.reshape(count, mode_count, rows_here, cols_here)
    far_re, far_im = halves(far_field)
    intensity = lax.optimization_barrier(jnp.sum(far_re * far_re + far_im * far_im, axis=1))
    scaling = amplitudes / jnp.maximum(jnp.sqrt(intensity), amp_floor)
    scaling = jnp.concatenate([scaling, scaling], -1)[:, None]
    corrected = (far_field * scaling).astype(jnp.bfloat16).reshape(count * mode_count, rows_here, cols_here)
    returned = left_apply(left_tables, corrected, -1.0).astype(jnp.bfloat16)
    near_field = jnp.einsum('bik,kl->bil', returned.astype(jnp.float32), right_inverse.astype(jnp.float32))
    change = near_field.reshape(count, mode_count, rows_here, cols_here) - exit_wave
    window_gradient = lax.optimization_barrier(jnp.sum(multiply(probe_full[None], change, True), axis=1))
    probe_gradient = lax.optimization_barrier(jnp.sum(multiply(windows[:, None], change, True), axis=0))
    return (window_gradient, probe_gradient)

def reference(object_field, probe_modes, measured, positions, subset_order):
    left_tables, right_forward, right_inverse = tables(W)
    subset_size = POS_DEV // SUBSETS
    probe_rate = 0.5 / POSITIONS
    tile_count = N_ROW * N_COL
    order_flat = subset_order.reshape(tile_count, POS_DEV)
    offset_flat = positions.reshape(tile_count, POS_DEV, 2)
    measured_flat = measured.reshape(tile_count, POS_DEV, W, W)
    for outer_step in range(OUTER):
        probe_total = jnp.zeros(probe_modes.shape, jnp.float32)
        for subset in range(SUBSETS):
            padded = jnp.pad(object_field, ((0, 0), (MARGIN, MARGIN), (MARGIN, MARGIN)))

            def visit_tile(state_pair, tile_id):
                grad_pad, probe_grad = state_pair
                tile_row = tile_id // N_COL * TILE
                tile_col = tile_id % N_COL * TILE
                chosen = order_flat[tile_id][subset * subset_size:(subset + 1) * subset_size]
                offsets = offset_flat[tile_id][chosen].astype(jnp.int32)
                amplitudes = measured_flat[tile_id][chosen]
                windows = []
                for member in range(subset_size):
                    window_planes = lax.dynamic_slice(padded, (jnp.int32(0), (tile_row + offsets[member, 0]).astype(jnp.int32), (tile_col + offsets[member, 1]).astype(jnp.int32)), (2, W, W))
                    windows.append(jnp.concatenate([window_planes[0], window_planes[1]], -1))
                windows = jnp.stack(windows)
                window_gradient, probe_part = project(windows, probe_modes, amplitudes, left_tables, right_forward, right_inverse)
                for member in range(subset_size):
                    grad_re, grad_im = halves(window_gradient[member])
                    starts = (jnp.int32(0), (tile_row + offsets[member, 0]).astype(jnp.int32), (tile_col + offsets[member, 1]).astype(jnp.int32))
                    current = lax.dynamic_slice(grad_pad, starts, (2, W, W))
                    grad_pad = lax.dynamic_update_slice(grad_pad, current + jnp.stack([grad_re, grad_im]), starts)
                return ((grad_pad, probe_grad + probe_part), None)
            start_pair = (jnp.zeros(padded.shape, jnp.float32), jnp.zeros(probe_modes.shape, jnp.float32))
            (grad_pad, probe_grad), _ = lax.scan(visit_tile, start_pair, jnp.arange(tile_count, dtype=jnp.int32))
            object_field = object_field + object_rate * grad_pad[:, MARGIN:MARGIN + NR, MARGIN:MARGIN + NC]
            probe_total = probe_total + probe_grad
        probe_modes = probe_modes + probe_rate * probe_total
    return (object_field, probe_modes)
```

```python
import functools
import math

import jax
import jax.numpy as jnp
import ml_dtypes
import numpy as np
from jax import lax
from jax.experimental import pallas as pl
from jax.experimental.pallas import tpu as pltpu
from jax.sharding import PartitionSpec as P

MARGIN = 64
SUBSETS = 2
OUTER = 2


amp_floor = 0.3
object_rate = 0.05


def extended_2(block, sides, width):
    for axis, dim in sides:
        count = lax.axis_size(axis)
        forward = [(i, i + 1) for i in range(count - 1)]
        backward = [(target, source) for source, target in forward]
        low = lax.ppermute(
            lax.slice_in_dim(block, block.shape[dim] - width, None, axis=dim), axis, forward
        )
        high = lax.ppermute(lax.slice_in_dim(block, 0, width, axis=dim), axis, backward)
        block = jnp.concatenate([low, block, high], axis=dim)
    return block


def tables(probe_size):
    ramp_values = jnp.arange(probe_size, dtype=jnp.int32)
    phases = ramp_values[:, None] * ramp_values[None, :] % probe_size
    angles = phases.astype(jnp.float32) * (2.0 * math.pi / probe_size)
    norming = 1.0 / math.sqrt(probe_size)
    cosine = jnp.cos(angles) * norming
    sine_part = jnp.sin(angles) * norming
    left_tables = jnp.stack([cosine, sine_part]).astype(jnp.bfloat16)
    right_forward = jnp.concatenate(
        [jnp.concatenate([cosine, -sine_part], 1), jnp.concatenate([sine_part, cosine], 1)], 0
    ).astype(jnp.bfloat16)
    right_inverse = jnp.concatenate(
        [jnp.concatenate([cosine, sine_part], 1), jnp.concatenate([-sine_part, cosine], 1)], 0
    ).astype(jnp.bfloat16)
    return (left_tables, right_forward, right_inverse)


def halves(values):
    middle = values.shape[-1] // 2
    return (values[..., :middle], values[..., middle:])


def multiply(former, latter, conjugate):
    former_re, former_im = halves(former)
    latter_re, latter_im = halves(latter)
    if conjugate:
        return jnp.concatenate(
            [
                former_re * latter_re + former_im * latter_im,
                former_re * latter_im - former_im * latter_re,
            ],
            -1,
        )
    return jnp.concatenate(
        [
            former_re * latter_re - former_im * latter_im,
            former_re * latter_im + former_im * latter_re,
        ],
        -1,
    )


def left_apply(left_tables, stacked, direction):
    products = jnp.einsum("tij,bjk->tbik", left_tables, stacked, preferred_element_type=jnp.float32)
    cos_re, cos_im = halves(products[0])
    sin_re, sin_im = halves(products[1])
    return jnp.concatenate([cos_re + direction * sin_im, cos_im - direction * sin_re], -1)


def project(windows, probe_full, amplitudes, left_tables, right_forward, right_inverse):
    exit_wave = multiply(probe_full[None], windows[:, None], False)
    count, mode_count, rows_here, cols_here = exit_wave.shape
    stacked = exit_wave.reshape(count * mode_count, rows_here, cols_here).astype(jnp.bfloat16)
    half_transform = left_apply(left_tables, stacked, 1.0).astype(jnp.bfloat16)
    far_field = jnp.einsum(
        "bik,kl->bil", half_transform, right_forward, preferred_element_type=jnp.float32
    )
    far_field = far_field.reshape(count, mode_count, rows_here, cols_here)
    far_re, far_im = halves(far_field)
    intensity = jnp.sum(far_re * far_re + far_im * far_im, axis=1)
    scaling = amplitudes / jnp.maximum(jnp.sqrt(intensity), amp_floor)
    scaling = jnp.concatenate([scaling, scaling], -1)[:, None]
    corrected = (
        (far_field * scaling).astype(jnp.bfloat16).reshape(count * mode_count, rows_here, cols_here)
    )
    returned = left_apply(left_tables, corrected, -1.0).astype(jnp.bfloat16)
    near_field = jnp.einsum(
        "bik,kl->bil", returned, right_inverse, preferred_element_type=jnp.float32
    )
    change = near_field.reshape(count, mode_count, rows_here, cols_here) - exit_wave
    window_gradient = jnp.sum(multiply(probe_full[None], change, True), axis=1)
    probe_gradient = jnp.sum(multiply(windows[:, None], change, True), axis=0)
    return (window_gradient, probe_gradient)


def spread(owned):
    gathered = lax.all_gather(owned, "col", axis=2, tiled=True)
    return lax.all_gather(gathered, "row", axis=1, tiled=True)


def fold(grad_extended, margin, tile_size):
    margins = jnp.concatenate(
        [grad_extended[:, :margin], grad_extended[:, tile_size + margin :]], 1
    )
    received = extended_2(margins, (("row", 1),), margin)
    interior = grad_extended[:, margin : margin + tile_size]
    interior = interior.at[:, :margin].add(received[:, :margin])
    interior = interior.at[:, tile_size - margin :].add(received[:, 3 * margin :])
    margins = jnp.concatenate([interior[:, :, :margin], interior[:, :, tile_size + margin :]], 2)
    received = extended_2(margins, (("col", 2),), margin)
    interior = interior[:, :, margin : margin + tile_size]
    interior = interior.at[:, :, :margin].add(received[:, :, :margin])
    interior = interior.at[:, :, tile_size - margin :].add(received[:, :, 3 * margin :])
    return interior


def shards(object_field, probe_modes, measured, positions, subset_order):
    probe_size = measured.shape[3]
    tile_size = object_field.shape[1]
    margin = MARGIN
    extent = tile_size + 2 * margin
    left_tables, right_forward, right_inverse = tables(probe_size)
    pos_count = subset_order.shape[2]
    subset_size = pos_count // SUBSETS
    probe_rate = 0.5 / (pos_count * lax.axis_size("row") * lax.axis_size("col"))
    probe_full = spread(probe_modes)
    for outer_step in range(OUTER):
        probe_total = jnp.zeros(probe_full.shape, jnp.float32)
        for subset in range(SUBSETS):
            extended = extended_2(object_field, (("row", 1), ("col", 2)), margin)
            chosen = subset_order[0, 0, subset * subset_size : (subset + 1) * subset_size]
            offsets = positions[0, 0][chosen]
            amplitudes = measured[0, 0][chosen]
            windows = []
            member = 0
            window_planes = lax.dynamic_slice(
                extended,
                (jnp.int32(0), offsets[member, 0], offsets[member, 1]),
                (2, probe_size, probe_size),
            )
            windows.append(jnp.concatenate([window_planes[0], window_planes[1]], -1))
            windows = jnp.stack(windows)
            window_gradient, probe_part = project(
                windows, probe_full, amplitudes, left_tables, right_forward, right_inverse
            )
            grad_extended = jnp.zeros((2, extent, extent), jnp.float32)
            member = 0
            grad_re, grad_im = halves(window_gradient[member])
            starts = (jnp.int32(0), offsets[member, 0], offsets[member, 1])
            grad_extended = lax.dynamic_update_slice(
                grad_extended, jnp.stack([grad_re, grad_im]), starts
            )
            object_field = object_field + object_rate * fold(grad_extended, margin, tile_size)
            probe_total = probe_total + probe_part
        owned_sum = lax.psum_scatter(probe_total, "row", scatter_dimension=1, tiled=True)
        owned_sum = lax.psum_scatter(owned_sum, "col", scatter_dimension=2, tiled=True)
        probe_modes = probe_modes + probe_rate * owned_sum
        if outer_step + 1 < OUTER:
            probe_full = spread(probe_modes)
    return (object_field, probe_modes)


LANES = 128


def host_tables(probe_size):
    ramp_values = np.arange(probe_size, dtype=np.int32)
    phases = ramp_values[:, None] * ramp_values[None, :] % probe_size
    angles = phases.astype(np.float32) * np.float32(2.0 * math.pi / probe_size)
    norming = np.float32(1.0 / math.sqrt(probe_size))
    cosine = np.cos(angles) * norming
    sine_part = np.sin(angles) * norming
    left_tables = np.stack([cosine, sine_part]).astype(ml_dtypes.bfloat16)
    right_forward = np.block([[cosine, -sine_part], [sine_part, cosine]]).astype(ml_dtypes.bfloat16)
    right_inverse = np.block([[cosine, sine_part], [-sine_part, cosine]]).astype(ml_dtypes.bfloat16)
    return (left_tables, right_forward, right_inverse)


def kernel(
    n_row, n_col, probe_rate,
    pos_ref, order_ref, obj_ref, prb_ref, meas_ref, lt_ref, rf_ref, ri_ref,
    out_obj, out_prb,
    ext, acc, gpad, win, ew, xb, zb, offs, roffs, srow, rrow, rcol,
    pf, pg, hs, rc, ry, ss, rr, ssem, rsem,
):
    r = lax.axis_index("row")
    c = lax.axis_index("col")
    tile = obj_ref.shape[1]
    width = meas_ref.shape[1]
    modes, pr, pw = prb_ref.shape
    margin = MARGIN
    strip = 2 * margin
    extent = tile + strip
    passes = OUTER * SUBSETS
    half = n_col // 2
    core = lax.rem(c, 2)
    q = lax.div(c, 2)
    sibling = c + 1 - 2 * core
    block = strip
    blocks = width // block
    pieces = block // pr
    f32 = jnp.float32
    ids = {}

    def sem_id(key):
        return ids.setdefault(key, len(ids))

    def copy(key, src, dst, device):
        index = sem_id(key)
        return pltpu.make_async_remote_copy(
            src_ref=src, dst_ref=dst, send_sem=ssem.at[index], recv_sem=rsem.at[index],
            device_id=device, device_id_type=pl.DeviceIdType.MESH,
        )

    barrier = pltpu.get_barrier_semaphore()
    for step in range(1, n_row):
        pl.semaphore_signal(
            barrier, inc=1, device_id=(lax.rem(r + step, n_row), c),
            device_id_type=pl.DeviceIdType.MESH,
        )
    for step in range(1, n_col):
        pl.semaphore_signal(
            barrier, inc=1, device_id=(r, lax.rem(c + step, n_col)),
            device_id_type=pl.DeviceIdType.MESH,
        )
    pl.semaphore_wait(barrier, n_row - 1 + n_col - 1)

    has_up, has_down = r > 0, r < n_row - 1
    has_left, has_right = c > 0, c < n_col - 1
    lanes = lax.broadcasted_iota(jnp.int32, (block, LANES), 1)


    def row_copy(e, side):
        if e == 0:
            rows = pl.ds(0, margin)
            src = obj_ref.at[:, pl.ds(0, margin)] if side == 0 else obj_ref.at[:, pl.ds(tile - margin, margin)]
        elif e == passes:
            rows = pl.ds(0, margin)
            src = srow.at[side, :, rows]
        else:
            src = srow.at[side]
            rows = pl.ds(0, strip)
        dst = rrow.at[e, 1 - side, :, rows]
        return copy(("row", e, side), src, dst, (r - 1 if side == 0 else r + 1, c))

    def col_copy(e, side, part):
        low, size = [(0, strip), (strip, tile - strip), (tile, strip)][part]
        if e == passes:
            low, size = [(margin, margin), (strip, tile - strip), (tile, margin)][part]
        rows = pl.ds(low, size)
        src = acc.at[2 * side, :, rows]
        dst = rcol.at[e, 1 - side, :, rows]
        return copy(("col", e, side, part), src, dst, (r, c - 1 if side == 0 else c + 1))

    def off_copy(side):
        return copy(("off", side), offs, roffs.at[1 - side], (r - 1 if side == 0 else r + 1, c))

    def start_cols(e, part):
        @pl.when(has_left)
        def _():
            col_copy(e, 0, part).start()

        @pl.when(has_right)
        def _():
            col_copy(e, 1, part).start()


    def ag_row(g, step):
        return copy(
            ("agr", g, step), pf.at[g, c, r], pf.at[g, c, r], (lax.rem(r + step, n_row), c)
        )

    def ag_sib(g, step):
        at = lax.rem(r + n_row - step, n_row)
        return copy(("ags", g, step), pf.at[g, c, at], pf.at[g, c, at], (r, sibling))

    def ag_par(g, step, other):
        at = lax.rem(r + n_row - step, n_row)
        to = 2 * lax.rem(q + other, half) + core
        return copy(("agp", g, step, other), pf.at[g, c, at], pf.at[g, c, at], (r, to))

    def ag_fwd(g, step, other):
        at = lax.rem(r + n_row - step, n_row)
        held = 2 * lax.rem(q + half - other, half) + core
        return copy(("agf", g, step, other), pf.at[g, held, at], pf.at[g, held, at], (r, sibling))

    def gather_send(g):
        for step in range(1, n_row):
            ag_row(g, step).start()
        ag_sib(g, 0).start()
        for other in range(1, half):
            ag_par(g, 0, other).start()

    def gather_pass_on(g):
        for step in range(1, n_row):
            ag_row(g, step).wait_recv()
            for other in range(1, half):
                ag_par(g, step, other).start()
            ag_sib(g, step).start()
        for step in range(n_row):
            for other in range(1, half):
                ag_par(g, step, other).wait_recv()
                ag_fwd(g, step, other).start()

    def gather_end(g):
        for step in range(n_row):
            ag_sib(g, step).wait_recv()
            for other in range(1, half):
                ag_fwd(g, step, other).wait_recv()
        for step in range(n_row):
            if step:
                ag_row(g, step).wait_send()
            ag_sib(g, step).wait_send()
            for other in range(1, half):
                ag_par(g, step, other).wait_send()
                ag_fwd(g, step, other).wait_send()


    def rs_core(t, k):
        return copy(("rsc", t, k), pg.at[2 * k + 1 - core], rc.at[t, k], (r, sibling))

    def rs_par(t, step, other):
        at = lax.rem(r + step, n_row)
        to_q = lax.rem(q + other, half)
        return copy(
            ("rsp", t, step, other), hs.at[to_q, at], ry.at[t, other, at], (r, 2 * to_q + core)
        )

    def rs_row(t, step):
        at = lax.rem(r + step, n_row)
        return copy(("rsr", t, step), ss.at[step], rr.at[t, step], (at, c))

    def sum_start(t):
        for k in range(half):
            rs_core(t, k).start()

    order = list(range(1, n_row)) + [0]

    def sum_pass_on(t):
        for k in range(half):
            rs_core(t, k).wait_recv()
        for step in order:
            at = lax.rem(r + step, n_row)
            for other in range(1, half):
                to_q = lax.rem(q + other, half)
                hs[to_q, at] = pg[2 * to_q + core, at] + rc[t, to_q, at]
                rs_par(t, step, other).start()
        for step in order:
            at = lax.rem(r + step, n_row)
            value = pg[c, at] + rc[t, q, at]
            for other in range(1, half):
                rs_par(t, step, other).wait_recv()
                value = value + ry[t, other, at]
            ss[step] = value
            if step:
                rs_row(t, step).start()

    def sum_end(t):
        value = ss[0]
        for step in range(1, n_row):
            rs_row(t, step).wait_recv()
            value = value + rr[t, step]
        return value

    def sum_sent(t):
        for k in range(half):
            rs_core(t, k).wait_send()
        for step in range(n_row):
            for other in range(1, half):
                rs_par(t, step, other).wait_send()
            if step:
                rs_row(t, step).wait_send()


    for subset in range(SUBSETS):
        offs[subset] = jnp.full(offs.shape[1:], pos_ref[order_ref[subset], 1], jnp.int32)

    @pl.when(has_up)
    def _():
        row_copy(0, 0).start()
        off_copy(0).start()

    @pl.when(has_down)
    def _():
        row_copy(0, 1).start()
        off_copy(1).start()

    pf[0, c, r] = prb_ref[...]
    gather_send(0)

    def placed(values):
        rows = values.shape[0]
        spot = lax.broadcasted_iota(jnp.int32, (rows, LANES), 1) >= margin
        first = pltpu.roll(values[:, :LANES], margin, 1)
        second = pltpu.roll(values[:, LANES:], margin, 1)
        zero = jnp.zeros_like(first)
        return (
            jnp.where(spot, first, zero), jnp.where(spot, second, first),
            jnp.where(spot, zero, second),
        )

    for plane in range(2):
        for k in range(2):
            gpad[plane, k, 0:strip] = jnp.zeros((strip, LANES), f32)
            gpad[plane, k, strip + width :] = jnp.zeros((strip, LANES), f32)
        for low in range(0, tile, margin):
            parts = placed(obj_ref[plane, low : low + margin])
            for b in range(3):
                acc[b, plane, margin + low : 2 * margin + low] = parts[b]
    start_cols(0, 1)

    def halo_rows(side, at):
        for plane in range(2):
            parts = placed(rrow[0, side, plane, 0:margin])
            for b in range(3):
                acc[b, plane, at : at + margin] = parts[b]

    def halo_zero(at):
        for plane in range(2):
            for b in range(3):
                acc[b, plane, at : at + margin] = jnp.zeros((margin, LANES), f32)

    @pl.when(has_down)
    def _():
        row_copy(0, 0).wait_recv()
        off_copy(0).wait_recv()
        halo_rows(1, tile + margin)

    @pl.when(jnp.logical_not(has_down))
    def _():
        halo_zero(tile + margin)

    start_cols(0, 2)

    @pl.when(has_up)
    def _():
        row_copy(0, 1).wait_recv()
        off_copy(1).wait_recv()
        halo_rows(0, 0)

    @pl.when(jnp.logical_not(has_up))
    def _():
        halo_zero(0)

    start_cols(0, 0)
    gather_pass_on(0)

    def take_cols(e):
        for part in range(3):
            @pl.when(has_left)
            def _():
                col_copy(e, 1, part).wait_recv()

            @pl.when(has_right)
            def _():
                col_copy(e, 0, part).wait_recv()

    def sent(e):
        @pl.when(has_up)
        def _():
            row_copy(e, 0).wait_send()

        @pl.when(has_down)
        def _():
            row_copy(e, 1).wait_send()

        for part in range(3):
            @pl.when(has_left)
            def _():
                col_copy(e, 0, part).wait_send()

            @pl.when(has_right)
            def _():
                col_copy(e, 1, part).wait_send()

    for side, there in ((0, has_left), (1, has_right)):
        @pl.when(jnp.logical_not(there))
        def _():
            for e in range(passes + 1):
                rcol[e, side] = jnp.zeros(rcol.shape[2:], f32)

    take_cols(0)
    for plane in range(2):
        ext[0, plane] = acc[0, plane] + rcol[0, 0, plane]
        ext[1, plane] = acc[1, plane]
        ext[2, plane] = acc[2, plane] + rcol[0, 1, plane]
    sent(0)

    @pl.when(has_up)
    def _():
        off_copy(0).wait_send()

    @pl.when(has_down)
    def _():
        off_copy(1).wait_send()

    gather_end(0)

    def probe_block(g, m, i):
        parts = [
            pf[g, k, pl.ds(i * pieces, pieces), m].reshape(block, pw) for k in range(n_col)
        ]
        return (
            jnp.concatenate(parts[:half], 1), jnp.concatenate(parts[half:], 1)
        )

    def gradient_rows(plane, low, size):
        return jnp.concatenate([gpad[plane, k, pl.ds(low, size), :] for k in range(2)], 1)

    def unpacked(mask, values):
        zero = jnp.zeros_like(values[:, :LANES])
        return (
            jnp.where(mask, values[:, :LANES], zero), values[:, LANES:],
            jnp.where(mask, zero, values[:, :LANES]),
        )

    row_low = jnp.where(has_up, 0, margin)
    row_high = jnp.where(has_down, extent, extent - margin)
    col_low = jnp.where(has_left, 0, margin)
    col_high = jnp.where(has_right, LANES, margin)

    for number in range(passes):
        outer_step, subset = number // SUBSETS, number % SUBSETS
        g = outer_step
        e = number + 1
        last = e == passes
        chosen = order_ref[subset]
        a = pos_ref[chosen, 0]
        b = pos_ref[chosen, 1]
        back = lax.rem(LANES - b, LANES)
        ahead = lax.rem(b, LANES)

        @pl.loop(0, blocks)
        def _(i):
            rows = pl.ds(pl.multiple_of(i * block, block), block)
            planes = []
            for plane in range(2):
                turned = [
                    pltpu.roll(ext[k, plane, pl.ds(a + i * block, block), :], back, 1)
                    for k in range(3)
                ]
                inside = lanes < LANES - b
                window = jnp.concatenate(
                    [jnp.where(inside, turned[k], turned[k + 1]) for k in range(2)], 1
                )
                win[plane, rows] = window
                planes.append(window)
            for m in range(modes):
                p_re, p_im = probe_block(g, m, i)
                wave = jnp.concatenate(
                    [p_re * planes[0] - p_im * planes[1], p_re * planes[1] + p_im * planes[0]], 1
                )
                ew[m, rows] = wave
                xb[m, rows] = wave.astype(jnp.bfloat16)

        def transform(source, m, rows, direction, table_ref):
            cos = jnp.dot(lt_ref[0, rows], source[m], preferred_element_type=f32)
            sin = jnp.dot(lt_ref[1, rows], source[m], preferred_element_type=f32)
            mixed = jnp.concatenate(
                [
                    cos[:, :width] + direction * sin[:, width:],
                    cos[:, width:] - direction * sin[:, :width],
                ],
                1,
            ).astype(jnp.bfloat16)
            return jnp.dot(mixed, table_ref[...], preferred_element_type=f32)

        @pl.loop(0, blocks)
        def _(i):
            rows = pl.ds(pl.multiple_of(i * block, block), block)
            far = [transform(xb, m, rows, 1.0, rf_ref) for m in range(modes)]
            intensity = sum(
                f[:, :width] * f[:, :width] + f[:, width:] * f[:, width:] for f in far
            )
            scaling = meas_ref[chosen, rows] * jnp.minimum(
                lax.rsqrt(intensity), 1.0 / amp_floor
            )
            scaling = jnp.concatenate([scaling, scaling], 1)
            for m in range(modes):
                zb[m, rows] = (far[m] * scaling).astype(jnp.bfloat16)

        mask = lanes >= b
        for i in range(blocks):
            rows = slice(i * block, (i + 1) * block)
            w_re, w_im = win[0, rows], win[1, rows]
            g_re = g_im = None
            for m in range(modes):
                change = transform(zb, m, rows, -1.0, ri_ref) - ew[m, rows]
                c_re, c_im = change[:, :width], change[:, width:]
                p_re, p_im = probe_block(g, m, i)
                part_re, part_im = p_re * c_re + p_im * c_im, p_re * c_im - p_im * c_re
                g_re = part_re if m == 0 else g_re + part_re
                g_im = part_im if m == 0 else g_im + part_im
                grad = jnp.concatenate(
                    [w_re * c_re + w_im * c_im, w_re * c_im - w_im * c_re], 1
                )
                at = slice(i * pieces, (i + 1) * pieces)
                for k in range(n_col):
                    value = grad[:, k * pw : (k + 1) * pw].reshape(pieces, pr, pw)
                    if subset:
                        value = value + pg[k, at, m]
                    pg[k, at, m] = value
            for plane, values in enumerate((g_re, g_im)):
                first = pltpu.roll(values[:, :LANES], ahead, 1)
                second = pltpu.roll(values[:, LANES:], ahead, 1)
                at = slice(strip + i * block, strip + (i + 1) * block)
                gpad[plane, 0, at] = jnp.where(mask, first, second)
                gpad[plane, 1, at] = jnp.where(mask, second, first)
            side = None
            if i == 0:
                side, there = 0, has_up
            elif i == blocks - 1:
                side, there = 1, has_down
            if side is not None:
                size = margin if last else strip
                low = strip if side == 0 else strip + extent - size
                for plane in range(2):
                    srow[side, plane, 0:size] = gradient_rows(plane, low - a, size)

                @pl.when(there)
                def _():
                    row_copy(e, side).start()

        if subset == SUBSETS - 1:
            sum_start(outer_step)

        for low in (strip, 0, tile):
            for plane in range(2):
                parts = unpacked(mask, gradient_rows(plane, strip + low - a, strip))
                for k in range(3):
                    acc[k, plane, low : low + strip] = parts[k]
            if low == strip:
                start_cols(e, 1)

        if subset == SUBSETS - 1:
            sum_pass_on(outer_step)

        def add_rows(side):
            size = margin if last else strip
            low = (margin if last else 0) if side == 0 else tile
            there = roffs[side, subset, 0:1, :]
            spot = lax.broadcasted_iota(jnp.int32, (size, LANES), 1) >= there
            for plane in range(2):
                parts = unpacked(spot, rrow[e, side, plane, 0:size])
                for k in range(3):
                    acc[k, plane, low : low + size] += parts[k]

        @pl.when(has_down)
        def _():
            row_copy(e, 0).wait_recv()
            add_rows(1)

        start_cols(e, 2)

        @pl.when(has_up)
        def _():
            row_copy(e, 1).wait_recv()
            add_rows(0)

        start_cols(e, 0)

        if subset == SUBSETS - 1:
            total = sum_end(outer_step)
            piece = (prb_ref[...] if outer_step == 0 else pf[g, c, r]) + probe_rate * total
            if last:
                out_prb[...] = piece
            else:
                pf[g + 1, c, r] = piece
                gather_send(g + 1)
                gather_pass_on(g + 1)

        take_cols(e)
        if not last:
            for low in range(0, extent, block):
                row_at = lax.broadcasted_iota(jnp.int32, (block, LANES), 0) + low
                good = jnp.logical_and(row_at >= row_low, row_at < row_high)
                rows = slice(low, low + block)
                for plane in range(2):
                    for k in range(3):
                        value = acc[k, plane, rows]
                        kept = good
                        if k == 0:
                            value = value + rcol[e, 0, plane, rows]
                            kept = jnp.logical_and(good, lanes >= col_low)
                        elif k == 2:
                            value = value + rcol[e, 1, plane, rows]
                            kept = jnp.logical_and(good, lanes < col_high)
                        ext[k, plane, rows] += jnp.where(
                            kept, object_rate * value, jnp.zeros_like(value)
                        )
        else:
            spot = lax.broadcasted_iota(jnp.int32, (margin, LANES), 1) < margin
            for low in range(0, tile, margin):
                rows = slice(margin + low, 2 * margin + low)
                for plane in range(2):
                    turned = []
                    for k in range(3):
                        value = acc[k, plane, rows]
                        if k != 1:
                            value = value + rcol[e, k // 2, plane, rows]
                        value = ext[k, plane, rows] + object_rate * value
                        turned.append(pltpu.roll(value, margin, 1))
                    out_obj[plane, low : low + margin] = jnp.concatenate(
                        [jnp.where(spot, turned[k], turned[k + 1]) for k in range(2)], 1
                    )
        sent(e)
        if subset == SUBSETS - 1:
            sum_sent(outer_step)
            if not last:
                gather_end(g + 1)


def tiles(object_field, probe_modes, measured, positions, subset_order):
    n_row, n_col = lax.axis_size("row"), lax.axis_size("col")
    tile = object_field.shape[1]
    modes, pr, pw = probe_modes.shape
    pos_count, width = measured.shape[2], measured.shape[3]
    strip = 2 * MARGIN
    fits = (
        pos_count == SUBSETS and strip == LANES and width == 2 * LANES and tile == width
        and n_col % 2 == 0 and pw == LANES and pr % 8 == 0 and strip % pr == 0
        and n_row > 1
    )
    if not fits:
        return shards(object_field, probe_modes, measured, positions, subset_order)
    extent = tile + strip
    passes = OUTER * SUBSETS
    half = n_col // 2
    probe_rate = 0.5 / (pos_count * n_row * n_col)
    left_tables, right_forward, right_inverse = host_tables(width)
    f32, bf16 = jnp.float32, jnp.bfloat16
    vmem = pl.BlockSpec(memory_space=pltpu.VMEM)
    smem = pl.BlockSpec(memory_space=pltpu.SMEM)
    copies = (passes + 1) * 8 + 2 + OUTER * n_row * 2 * n_col + OUTER * n_row * n_col
    return pl.pallas_call(
        functools.partial(kernel, n_row, n_col, probe_rate),
        out_shape=(
            jax.ShapeDtypeStruct(object_field.shape, f32),
            jax.ShapeDtypeStruct(probe_modes.shape, f32),
        ),
        in_specs=[smem, smem] + [vmem] * 6,
        out_specs=(vmem, vmem),
        scratch_shapes=[
            pltpu.VMEM((3, 2, extent, LANES), f32),
            pltpu.VMEM((3, 2, extent, LANES), f32),
            pltpu.VMEM((2, 2, width + 2 * strip, LANES), f32),
            pltpu.VMEM((2, width, width), f32),
            pltpu.VMEM((modes, width, 2 * width), f32),
            pltpu.VMEM((modes, width, 2 * width), bf16),
            pltpu.VMEM((modes, width, 2 * width), bf16),
            pltpu.VMEM((SUBSETS, 8, LANES), jnp.int32),
            pltpu.VMEM((2, SUBSETS, 8, LANES), jnp.int32),
            pltpu.VMEM((2, 2, strip, width), f32),
            pltpu.VMEM((passes + 1, 2, 2, strip, width), f32),
            pltpu.VMEM((passes + 1, 2, 2, extent, LANES), f32),
            pltpu.VMEM((OUTER, n_col, n_row, modes, pr, pw), f32),
            pltpu.VMEM((n_col, n_row, modes, pr, pw), f32),
            pltpu.VMEM((half, n_row, modes, pr, pw), f32),
            pltpu.VMEM((OUTER, half, n_row, modes, pr, pw), f32),
            pltpu.VMEM((OUTER, half, n_row, modes, pr, pw), f32),
            pltpu.VMEM((n_row, modes, pr, pw), f32),
            pltpu.VMEM((OUTER, n_row, modes, pr, pw), f32),
            pltpu.SemaphoreType.DMA((copies,)),
            pltpu.SemaphoreType.DMA((copies,)),
        ],
        compiler_params=pltpu.CompilerParams(
            collective_id=0, has_side_effects=True, vmem_limit_bytes=48 * 1024 * 1024
        ),
    )(
        positions[0, 0], subset_order[0, 0], object_field, probe_modes, measured[0, 0],
        jnp.asarray(left_tables), jnp.asarray(right_forward), jnp.asarray(right_inverse),
    )


def solution(mesh):
    in_specs = (
        P(None, "row", "col"),
        P(None, "row", "col"),
        P("row", "col", None, None, None),
        P("row", "col", None, None),
        P("row", "col", None),
    )
    out_specs = (P(None, "row", "col"), P(None, "row", "col"))
    return jax.shard_map(tiles, mesh=mesh, in_specs=in_specs, out_specs=out_specs, check_vma=False)
```

```python
import functools
import math

import jax
import jax.numpy as jnp
import ml_dtypes
import numpy as np
from jax import lax
from jax.experimental import pallas as pl
from jax.experimental.pallas import tpu as pltpu
from jax.sharding import PartitionSpec as P

MARGIN = 64
SUBSETS = 2
OUTER = 2


amp_floor = 0.3
object_rate = 0.05


def extended_2(block, sides, width):
    for axis, dim in sides:
        count = lax.axis_size(axis)
        forward = [(i, i + 1) for i in range(count - 1)]
        backward = [(target, source) for source, target in forward]
        low = lax.ppermute(
            lax.slice_in_dim(block, block.shape[dim] - width, None, axis=dim), axis, forward
        )
        high = lax.ppermute(lax.slice_in_dim(block, 0, width, axis=dim), axis, backward)
        block = jnp.concatenate([low, block, high], axis=dim)
    return block


def tables(probe_size):
    ramp_values = jnp.arange(probe_size, dtype=jnp.int32)
    phases = ramp_values[:, None] * ramp_values[None, :] % probe_size
    angles = phases.astype(jnp.float32) * (2.0 * math.pi / probe_size)
    norming = 1.0 / math.sqrt(probe_size)
    cosine = jnp.cos(angles) * norming
    sine_part = jnp.sin(angles) * norming
    left_tables = jnp.stack([cosine, sine_part]).astype(jnp.bfloat16)
    right_forward = jnp.concatenate(
        [jnp.concatenate([cosine, -sine_part], 1), jnp.concatenate([sine_part, cosine], 1)], 0
    ).astype(jnp.bfloat16)
    right_inverse = jnp.concatenate(
        [jnp.concatenate([cosine, sine_part], 1), jnp.concatenate([-sine_part, cosine], 1)], 0
    ).astype(jnp.bfloat16)
    return (left_tables, right_forward, right_inverse)


def halves(values):
    middle = values.shape[-1] // 2
    return (values[..., :middle], values[..., middle:])


def multiply(former, latter, conjugate):
    former_re, former_im = halves(former)
    latter_re, latter_im = halves(latter)
    if conjugate:
        return jnp.concatenate(
            [
                former_re * latter_re + former_im * latter_im,
                former_re * latter_im - former_im * latter_re,
            ],
            -1,
        )
    return jnp.concatenate(
        [
            former_re * latter_re - former_im * latter_im,
            former_re * latter_im + former_im * latter_re,
        ],
        -1,
    )


def left_apply(left_tables, stacked, direction):
    products = jnp.einsum("tij,bjk->tbik", left_tables, stacked, preferred_element_type=jnp.float32)
    cos_re, cos_im = halves(products[0])
    sin_re, sin_im = halves(products[1])
    return jnp.concatenate([cos_re + direction * sin_im, cos_im - direction * sin_re], -1)


def project(windows, probe_full, amplitudes, left_tables, right_forward, right_inverse):
    exit_wave = multiply(probe_full[None], windows[:, None], False)
    count, mode_count, rows_here, cols_here = exit_wave.shape
    stacked = exit_wave.reshape(count * mode_count, rows_here, cols_here).astype(jnp.bfloat16)
    half_transform = left_apply(left_tables, stacked, 1.0).astype(jnp.bfloat16)
    far_field = jnp.einsum(
        "bik,kl->bil", half_transform, right_forward, preferred_element_type=jnp.float32
    )
    far_field = far_field.reshape(count, mode_count, rows_here, cols_here)
    far_re, far_im = halves(far_field)
    intensity = jnp.sum(far_re * far_re + far_im * far_im, axis=1)
    scaling = amplitudes / jnp.maximum(jnp.sqrt(intensity), amp_floor)
    scaling = jnp.concatenate([scaling, scaling], -1)[:, None]
    corrected = (
        (far_field * scaling).astype(jnp.bfloat16).reshape(count * mode_count, rows_here, cols_here)
    )
    returned = left_apply(left_tables, corrected, -1.0).astype(jnp.bfloat16)
    near_field = jnp.einsum(
        "bik,kl->bil", returned, right_inverse, preferred_element_type=jnp.float32
    )
    change = near_field.reshape(count, mode_count, rows_here, cols_here) - exit_wave
    window_gradient = jnp.sum(multiply(probe_full[None], change, True), axis=1)
    probe_gradient = jnp.sum(multiply(windows[:, None], change, True), axis=0)
    return (window_gradient, probe_gradient)


def spread(owned):
    gathered = lax.all_gather(owned, "col", axis=2, tiled=True)
    return lax.all_gather(gathered, "row", axis=1, tiled=True)


def fold(grad_extended, margin, tile_size):
    margins = jnp.concatenate(
        [grad_extended[:, :margin], grad_extended[:, tile_size + margin :]], 1
    )
    received = extended_2(margins, (("row", 1),), margin)
    interior = grad_extended[:, margin : margin + tile_size]
    interior = interior.at[:, :margin].add(received[:, :margin])
    interior = interior.at[:, tile_size - margin :].add(received[:, 3 * margin :])
    margins = jnp.concatenate([interior[:, :, :margin], interior[:, :, tile_size + margin :]], 2)
    received = extended_2(margins, (("col", 2),), margin)
    interior = interior[:, :, margin : margin + tile_size]
    interior = interior.at[:, :, :margin].add(received[:, :, :margin])
    interior = interior.at[:, :, tile_size - margin :].add(received[:, :, 3 * margin :])
    return interior


def shards(object_field, probe_modes, measured, positions, subset_order):
    probe_size = measured.shape[3]
    tile_size = object_field.shape[1]
    margin = MARGIN
    extent = tile_size + 2 * margin
    left_tables, right_forward, right_inverse = tables(probe_size)
    pos_count = subset_order.shape[2]
    subset_size = pos_count // SUBSETS
    probe_rate = 0.5 / (pos_count * lax.axis_size("row") * lax.axis_size("col"))
    probe_full = spread(probe_modes)
    for outer_step in range(OUTER):
        probe_total = jnp.zeros(probe_full.shape, jnp.float32)
        for subset in range(SUBSETS):
            extended = extended_2(object_field, (("row", 1), ("col", 2)), margin)
            chosen = subset_order[0, 0, subset * subset_size : (subset + 1) * subset_size]
            offsets = positions[0, 0][chosen]
            amplitudes = measured[0, 0][chosen]
            windows = []
            member = 0
            window_planes = lax.dynamic_slice(
                extended,
                (jnp.int32(0), offsets[member, 0], offsets[member, 1]),
                (2, probe_size, probe_size),
            )
            windows.append(jnp.concatenate([window_planes[0], window_planes[1]], -1))
            windows = jnp.stack(windows)
            window_gradient, probe_part = project(
                windows, probe_full, amplitudes, left_tables, right_forward, right_inverse
            )
            grad_extended = jnp.zeros((2, extent, extent), jnp.float32)
            member = 0
            grad_re, grad_im = halves(window_gradient[member])
            starts = (jnp.int32(0), offsets[member, 0], offsets[member, 1])
            grad_extended = lax.dynamic_update_slice(
                grad_extended, jnp.stack([grad_re, grad_im]), starts
            )
            object_field = object_field + object_rate * fold(grad_extended, margin, tile_size)
            probe_total = probe_total + probe_part
        owned_sum = lax.psum_scatter(probe_total, "row", scatter_dimension=1, tiled=True)
        owned_sum = lax.psum_scatter(owned_sum, "col", scatter_dimension=2, tiled=True)
        probe_modes = probe_modes + probe_rate * owned_sum
        if outer_step + 1 < OUTER:
            probe_full = spread(probe_modes)
    return (object_field, probe_modes)


LANES = 128


def host_tables(probe_size):
    ramp_values = np.arange(probe_size, dtype=np.int32)
    phases = ramp_values[:, None] * ramp_values[None, :] % probe_size
    angles = phases.astype(np.float32) * np.float32(2.0 * math.pi / probe_size)
    norming = np.float32(1.0 / math.sqrt(probe_size))
    cosine = np.cos(angles) * norming
    sine_part = np.sin(angles) * norming
    left_tables = np.stack([cosine, sine_part]).astype(ml_dtypes.bfloat16)
    right_forward = np.block([[cosine, -sine_part], [sine_part, cosine]]).astype(ml_dtypes.bfloat16)
    right_inverse = np.block([[cosine, sine_part], [-sine_part, cosine]]).astype(ml_dtypes.bfloat16)
    return (left_tables, right_forward, right_inverse)


def kernel(
    n_row, n_col, probe_rate,
    pos_ref, order_ref, obj_far, prb_ref, meas_far, lt_far, rf_far, ri_far,
    out_obj, out_prb,
    ext, acc, gpad, win, ew, xb, zb, offs, roffs, srow, rrow, rnear, rfar, rcol,
    pf, pg, hs, rc, ry, sx, rx, ss, rr,
    obj_ref, meas_ref, lt_ref, rf_ref, ri_ref, ssem, rsem, lsem,
):
    r = lax.axis_index("row")
    c = lax.axis_index("col")
    tile = obj_far.shape[1]
    width = meas_far.shape[1]
    modes, pr, pw = prb_ref.shape
    margin = MARGIN
    strip = 2 * margin
    extent = tile + strip
    passes = OUTER * SUBSETS
    half = n_col // 2
    core = lax.rem(c, 2)
    q = lax.div(c, 2)
    sibling = c + 1 - 2 * core
    block = strip
    blocks = width // block
    pieces = block // pr
    f32 = jnp.float32
    ids = {}

    def sem_id(key):
        return ids.setdefault(key, len(ids))

    def copy(key, src, dst, device):
        index = sem_id(key)
        return pltpu.make_async_remote_copy(
            src_ref=src, dst_ref=dst, send_sem=ssem.at[index], recv_sem=rsem.at[index],
            device_id=device, device_id_type=pl.DeviceIdType.MESH,
        )

    nz = n_row // 2
    z = lax.div(r, 2)
    odd = lax.rem(r, 2)
    pair = r + 1 - 2 * odd

    loads = [
        pltpu.make_async_copy(src, dst, lsem.at[index])
        for index, (src, dst) in enumerate(
            (
                (obj_far, obj_ref), (lt_far, lt_ref), (rf_far, rf_ref), (meas_far, meas_ref),
                (ri_far, ri_ref), (prb_ref, pf.at[0, c, r]),
            )
        )
    ]
    for load in loads:
        load.start()

    barrier = pltpu.get_barrier_semaphore()
    for step in range(1, n_row):
        pl.semaphore_signal(
            barrier, inc=1, device_id=(lax.rem(r + step, n_row), c),
            device_id_type=pl.DeviceIdType.MESH,
        )
    for step in range(1, n_col):
        pl.semaphore_signal(
            barrier, inc=1, device_id=(r, lax.rem(c + step, n_col)),
            device_id_type=pl.DeviceIdType.MESH,
        )
    pl.semaphore_wait(barrier, n_row - 1 + n_col - 1)

    has_up, has_down = r > 0, r < n_row - 1
    has_left, has_right = c > 0, c < n_col - 1
    lanes = lax.broadcasted_iota(jnp.int32, (block, LANES), 1)


    def row_copy(e, side):
        low = 0 if side == 0 else tile - margin
        src = obj_far.at[:, pl.ds(low, margin)]
        return copy(
            ("row", e, side), src, rrow.at[1 - side], (r - 1 if side == 0 else r + 1, c)
        )

    def chunks(e):
        return 2 if e == passes else 2 * (strip // margin)

    def near_copy(e, j):
        return copy(("near", e, j), srow.at[j], rnear.at[e - 1, j], (pair, c))

    def far_copy(e, j):
        to = jnp.where(odd == 1, r - 2, r + 2)
        return copy(("far", e, j), rnear.at[e - 1, j], rfar.at[e - 1, j], (to, c))

    even = odd == 0
    takes_far = jnp.logical_or(
        jnp.logical_and(even, has_up), jnp.logical_and(jnp.logical_not(even), has_down)
    )
    gives_far = jnp.logical_or(
        jnp.logical_and(even, r < n_row - 2), jnp.logical_and(jnp.logical_not(even), r > 1)
    )

    def strip_low(e, part):
        top = margin if e == passes else 0
        if part == 0:
            return pl.multiple_of(jnp.where(even, tile, top), margin)
        return pl.multiple_of(jnp.where(even, top, tile), margin)

    def col_copy(e, side, part):
        if part == 1:
            low, size = strip, tile - strip
        elif e == 0:
            low, size = (0, tile)[part // 2], strip
        else:
            low, size = strip_low(e, part), margin if e == passes else strip
        rows = pl.ds(low, size)
        src = acc.at[2 * side, :, rows]
        dst = rcol.at[e, 1 - side, :, rows]
        return copy(("col", e, side, part), src, dst, (r, c - 1 if side == 0 else c + 1))

    def off_copy(side):
        return copy(("off", side), offs, roffs.at[1 - side], (r - 1 if side == 0 else r + 1, c))

    def start_cols(e, part):
        @pl.when(has_left)
        def _():
            col_copy(e, 0, part).start()

        @pl.when(has_right)
        def _():
            col_copy(e, 1, part).start()


    def piece_at(step, other_half, sign):
        place = 2 * lax.rem(z + (step if sign > 0 else nz - step), nz)
        return place + (1 - odd if other_half else odd)

    def own_or(g, held, step, other_half):
        if g == 0 and step == 0 and other_half == 0:
            return prb_ref
        return pf.at[g, held, piece_at(step, other_half, -1)]

    def ag_z(g, step):
        to = 2 * lax.rem(z + step, nz) + odd
        return copy(("agz", g, step), own_or(g, c, 0, 0), pf.at[g, c, r], (to, c))

    def ag_x(g, step):
        at = piece_at(step, 0, -1)
        return copy(("agx", g, step), own_or(g, c, step, 0), pf.at[g, c, at], (pair, c))

    def ag_sib(g, step, s):
        at = piece_at(step, s, -1)
        return copy(("ags", g, step, s), own_or(g, c, step, s), pf.at[g, c, at], (r, sibling))

    def ag_par(g, step, s, other):
        at = piece_at(step, s, -1)
        to = 2 * lax.rem(q + other, half) + core
        return copy(("agp", g, step, s, other), own_or(g, c, step, s), pf.at[g, c, at], (r, to))

    def ag_fwd(g, step, s, other):
        at = piece_at(step, s, -1)
        held = 2 * lax.rem(q + half - other, half) + core
        return copy(
            ("agf", g, step, s, other), pf.at[g, held, at], pf.at[g, held, at], (r, sibling)
        )

    def hand_on(g, step, s):
        for other in range(1, half):
            ag_par(g, step, s, other).start()
        ag_sib(g, step, s).start()

    def gather_send(g):
        for step in range(1, nz):
            ag_z(g, step).start()
        ag_x(g, 0).start()
        hand_on(g, 0, 0)

    def gather_pass_on(g):
        for step in range(1, nz):
            ag_z(g, step).wait_recv()
            ag_x(g, step).start()
            hand_on(g, step, 0)
        for step in range(nz):
            ag_x(g, step).wait_recv()
            hand_on(g, step, 1)
        for s in range(2):
            for step in range(nz):
                for other in range(1, half):
                    ag_par(g, step, s, other).wait_recv()
                    ag_fwd(g, step, s, other).start()

    def gather_end(g):
        for s in range(2):
            for step in range(nz):
                ag_sib(g, step, s).wait_recv()
                for other in range(1, half):
                    ag_fwd(g, step, s, other).wait_recv()
        for step in range(nz):
            if step:
                ag_z(g, step).wait_send()
            ag_x(g, step).wait_send()
            for s in range(2):
                ag_sib(g, step, s).wait_send()
                for other in range(1, half):
                    ag_par(g, step, s, other).wait_send()
                    ag_fwd(g, step, s, other).wait_send()


    def rs_core(t, k, i):
        at = pl.ds(i * pieces, pieces)
        return copy(
            ("rsc", t, k, i), pg.at[2 * k + 1 - core, at], rc.at[t, k, at], (r, sibling)
        )

    def rs_par(t, step, s, other):
        at = piece_at(step, s, 1)
        to_q = lax.rem(q + other, half)
        return copy(
            ("rsp", t, step, s, other), hs.at[to_q, at], ry.at[t, other, at],
            (r, 2 * to_q + core),
        )

    def rs_x(t, step):
        return copy(("rsx", t, step), sx.at[step], rx.at[t, step], (pair, c))

    def rs_z(t, step):
        to = 2 * lax.rem(z + step, nz) + odd
        return copy(("rsz", t, step), ss.at[step], rr.at[t, step], (to, c))

    def sum_start(t, i):
        for k in range(half):
            rs_core(t, k, i).start()

    order = list(range(1, nz)) + [0]

    def sum_pass_on(t):
        for i in range(blocks):
            for k in range(half):
                rs_core(t, k, i).wait_recv()
        for s in (1, 0):
            for step in order:
                at = piece_at(step, s, 1)
                for other in range(1, half):
                    to_q = lax.rem(q + other, half)
                    hs[to_q, at] = pg[2 * to_q + core, at] + rc[t, to_q, at]
                    rs_par(t, step, s, other).start()

    def sum_piece(t, step, s):
        at = piece_at(step, s, 1)
        value = pg[c, at] + rc[t, q, at]
        for other in range(1, half):
            rs_par(t, step, s, other).wait_recv()
            value = value + ry[t, other, at]
        return value

    def sum_across(t):
        for step in order:
            sx[step] = sum_piece(t, step, 1)
            rs_x(t, step).start()
        for step in order:
            value = sum_piece(t, step, 0)
            rs_x(t, step).wait_recv()
            ss[step] = value + rx[t, step]
            if step:
                rs_z(t, step).start()

    def sum_end(t):
        value = ss[0]
        for step in range(1, nz):
            rs_z(t, step).wait_recv()
            value = value + rr[t, step]
        return value

    def sum_sent(t):
        for i in range(blocks):
            for k in range(half):
                rs_core(t, k, i).wait_send()
        for step in range(nz):
            for s in range(2):
                for other in range(1, half):
                    rs_par(t, step, s, other).wait_send()
            rs_x(t, step).wait_send()
            if step:
                rs_z(t, step).wait_send()


    for subset in range(SUBSETS):
        for d in range(2):
            offs[subset, d] = jnp.full(
                offs.shape[2:], pos_ref[order_ref[subset], d], jnp.int32
            )

    @pl.when(has_up)
    def _():
        row_copy(0, 0).start()
        off_copy(0).start()

    @pl.when(has_down)
    def _():
        row_copy(0, 1).start()
        off_copy(1).start()

    gather_send(0)
    loads[0].wait()

    def placed(values):
        rows = values.shape[0]
        spot = lax.broadcasted_iota(jnp.int32, (rows, LANES), 1) >= margin
        first = pltpu.roll(values[:, :LANES], margin, 1)
        second = pltpu.roll(values[:, LANES:], margin, 1)
        zero = jnp.zeros_like(first)
        return (
            jnp.where(spot, first, zero), jnp.where(spot, second, first),
            jnp.where(spot, zero, second),
        )

    for plane in range(2):
        for k in range(2):
            gpad[plane, k, 0:strip] = jnp.zeros((strip, LANES), f32)
            gpad[plane, k, strip + width :] = jnp.zeros((strip, LANES), f32)
        for low in range(0, tile, margin):
            parts = placed(obj_ref[plane, low : low + margin])
            for b in range(3):
                acc[b, plane, margin + low : 2 * margin + low] = parts[b]
    start_cols(0, 1)

    def halo_rows(side, at):
        for plane in range(2):
            parts = placed(rrow[side, plane])
            for b in range(3):
                acc[b, plane, at : at + margin] = parts[b]

    def halo_zero(at):
        for plane in range(2):
            for b in range(3):
                acc[b, plane, at : at + margin] = jnp.zeros((margin, LANES), f32)

    @pl.when(has_down)
    def _():
        row_copy(0, 0).wait_recv()
        off_copy(0).wait_recv()
        halo_rows(1, tile + margin)

    @pl.when(jnp.logical_not(has_down))
    def _():
        halo_zero(tile + margin)

    start_cols(0, 2)

    @pl.when(has_up)
    def _():
        row_copy(0, 1).wait_recv()
        off_copy(1).wait_recv()
        halo_rows(0, 0)

    @pl.when(jnp.logical_not(has_up))
    def _():
        halo_zero(0)

    start_cols(0, 0)
    gather_pass_on(0)

    def take_cols(e):
        for part in range(3):
            @pl.when(has_left)
            def _():
                col_copy(e, 1, part).wait_recv()

            @pl.when(has_right)
            def _():
                col_copy(e, 0, part).wait_recv()

    def sent(e):
        if e == 0:
            @pl.when(has_up)
            def _():
                row_copy(e, 0).wait_send()

            @pl.when(has_down)
            def _():
                row_copy(e, 1).wait_send()
        else:
            for j in range(chunks(e)):
                near_copy(e, j).wait_send()

            @pl.when(gives_far)
            def _():
                for j in range(chunks(e)):
                    far_copy(e, j).wait_send()

        for part in range(3):
            @pl.when(has_left)
            def _():
                col_copy(e, 0, part).wait_send()

            @pl.when(has_right)
            def _():
                col_copy(e, 1, part).wait_send()

    for side, there in ((0, has_left), (1, has_right)):
        @pl.when(jnp.logical_not(there))
        def _():
            for e in range(passes + 1):
                rcol[e, side] = jnp.zeros(rcol.shape[2:], f32)

    take_cols(0)
    for plane in range(2):
        ext[0, plane] = acc[0, plane] + rcol[0, 0, plane]
        ext[1, plane] = acc[1, plane]
        ext[2, plane] = acc[2, plane] + rcol[0, 1, plane]
    sent(0)

    @pl.when(has_up)
    def _():
        off_copy(0).wait_send()

    @pl.when(has_down)
    def _():
        off_copy(1).wait_send()

    gather_end(0)
    for load in loads[1:]:
        load.wait()

    def probe_block(g, m, i):
        parts = [
            pf[g, k, pl.ds(i * pieces, pieces), m].reshape(block, pw) for k in range(n_col)
        ]
        return (
            jnp.concatenate(parts[:half], 1), jnp.concatenate(parts[half:], 1)
        )

    def gradient_rows(plane, low, size):
        return jnp.concatenate([gpad[plane, k, pl.ds(low, size), :] for k in range(2)], 1)

    def unpacked(mask, values):
        zero = jnp.zeros_like(values[:, :LANES])
        return (
            jnp.where(mask, values[:, :LANES], zero), values[:, LANES:],
            jnp.where(mask, zero, values[:, :LANES]),
        )

    row_low = jnp.where(has_up, 0, margin)
    row_high = jnp.where(has_down, extent, extent - margin)
    col_low = jnp.where(has_left, 0, margin)
    col_high = jnp.where(has_right, LANES, margin)

    for number in range(passes):
        outer_step, subset = number // SUBSETS, number % SUBSETS
        g = outer_step
        e = number + 1
        last = e == passes
        chosen = order_ref[subset]
        a = pos_ref[chosen, 0]
        b = pos_ref[chosen, 1]
        back = lax.rem(LANES - b, LANES)
        ahead = lax.rem(b, LANES)

        @pl.loop(0, blocks)
        def _(i):
            rows = pl.ds(pl.multiple_of(i * block, block), block)
            planes = []
            for plane in range(2):
                turned = [
                    pltpu.roll(ext[k, plane, pl.ds(a + i * block, block), :], back, 1)
                    for k in range(3)
                ]
                inside = lanes < LANES - b
                window = jnp.concatenate(
                    [jnp.where(inside, turned[k], turned[k + 1]) for k in range(2)], 1
                )
                win[plane, rows] = window
                planes.append(window)
            for m in range(modes):
                p_re, p_im = probe_block(g, m, i)
                wave = jnp.concatenate(
                    [p_re * planes[0] - p_im * planes[1], p_re * planes[1] + p_im * planes[0]], 1
                )
                ew[m, rows] = wave
                xb[m, rows] = wave.astype(jnp.bfloat16)

        def transform(source, m, rows, direction, table_ref):
            cos = jnp.dot(lt_ref[0, rows], source[m], preferred_element_type=f32)
            sin = jnp.dot(lt_ref[1, rows], source[m], preferred_element_type=f32)
            mixed = jnp.concatenate(
                [
                    cos[:, :width] + direction * sin[:, width:],
                    cos[:, width:] - direction * sin[:, :width],
                ],
                1,
            ).astype(jnp.bfloat16)
            return jnp.dot(mixed, table_ref[...], preferred_element_type=f32)

        @pl.loop(0, blocks)
        def _(i):
            rows = pl.ds(pl.multiple_of(i * block, block), block)
            far = [transform(xb, m, rows, 1.0, rf_ref) for m in range(modes)]
            intensity = sum(
                f[:, :width] * f[:, :width] + f[:, width:] * f[:, width:] for f in far
            )
            scaling = meas_ref[chosen, rows] * jnp.minimum(
                lax.rsqrt(intensity), 1.0 / amp_floor
            )
            scaling = jnp.concatenate([scaling, scaling], 1)
            for m in range(modes):
                zb[m, rows] = (far[m] * scaling).astype(jnp.bfloat16)

        mask = lanes >= b
        for i in range(blocks):
            rows = slice(i * block, (i + 1) * block)
            w_re, w_im = win[0, rows], win[1, rows]
            g_re = g_im = None
            for m in range(modes):
                change = transform(zb, m, rows, -1.0, ri_ref) - ew[m, rows]
                c_re, c_im = change[:, :width], change[:, width:]
                p_re, p_im = probe_block(g, m, i)
                part_re, part_im = p_re * c_re + p_im * c_im, p_re * c_im - p_im * c_re
                g_re = part_re if m == 0 else g_re + part_re
                g_im = part_im if m == 0 else g_im + part_im
                grad = jnp.concatenate(
                    [w_re * c_re + w_im * c_im, w_re * c_im - w_im * c_re], 1
                )
                at = slice(i * pieces, (i + 1) * pieces)
                for k in range(n_col):
                    value = grad[:, k * pw : (k + 1) * pw].reshape(pieces, pr, pw)
                    if subset:
                        value = value + pg[k, at, m]
                    pg[k, at, m] = value
            for plane, values in enumerate((g_re, g_im)):
                first = pltpu.roll(values[:, :LANES], ahead, 1)
                second = pltpu.roll(values[:, LANES:], ahead, 1)
                at = slice(strip + i * block, strip + (i + 1) * block)
                gpad[plane, 0, at] = jnp.where(mask, first, second)
                gpad[plane, 1, at] = jnp.where(mask, second, first)
            if subset == SUBSETS - 1:
                sum_start(outer_step, i)

        for j in range(chunks(e)):
            if last:
                plane, top, bottom = j, 0, extent - margin
            else:
                plane, top = j // 2, j % 2 * margin
                bottom = tile + top
            srow[j] = gradient_rows(plane, strip + top - a, margin) + gradient_rows(
                plane, strip + bottom - a, margin
            )
            near_copy(e, j).start()

        for low in (strip, 0, tile):
            for plane in range(2):
                parts = unpacked(mask, gradient_rows(plane, strip + low - a, strip))
                for k in range(3):
                    acc[k, plane, low : low + strip] = parts[k]
            if low == strip:
                start_cols(e, 1)

        def add_rows(part, take, arrived):
            from_down = even if part == 0 else jnp.logical_not(even)
            side = jnp.where(from_down, 1, 0)
            low = strip_low(e, part)
            there_a, there_b = roffs[side, subset, 0, 0:1, :], roffs[side, subset, 1, 0:1, :]
            spot = lax.broadcasted_iota(jnp.int32, (margin, LANES), 1) >= there_b
            row_at = lax.broadcasted_iota(jnp.int32, (margin, LANES), 0)
            for j in range(chunks(e)):
                take(e, j).wait_recv()
                plane, top = (j, 0) if last else (j // 2, j % 2 * margin)
                under = row_at + (margin if last else top)
                kept = jnp.where(from_down, row_at + top - there_a, there_a - 1 - under) >= 0
                values = arrived[e - 1, j]
                values = jnp.where(
                    jnp.concatenate([kept, kept], 1), values, jnp.zeros_like(values)
                )
                parts = unpacked(spot, values)
                rows = pl.ds(pl.multiple_of(low + top, margin), margin)
                for k in range(3):
                    acc[k, plane, rows] += parts[k]
                if part == 0:
                    @pl.when(gives_far)
                    def _():
                        far_copy(e, j).start()

        if subset == SUBSETS - 1:
            sum_pass_on(outer_step)
        add_rows(0, near_copy, rnear)
        start_cols(e, 0)
        if subset == SUBSETS - 1:
            sum_across(outer_step)

        @pl.when(takes_far)
        def _():
            add_rows(2, far_copy, rfar)

        start_cols(e, 2)

        if subset == SUBSETS - 1:
            total = sum_end(outer_step)
            piece = pf[g, c, r] + probe_rate * total
            if last:
                out_prb[...] = piece
            else:
                pf[g + 1, c, r] = piece
                gather_send(g + 1)
                gather_pass_on(g + 1)

        take_cols(e)
        if not last:
            for low in range(0, extent, block):
                row_at = lax.broadcasted_iota(jnp.int32, (block, LANES), 0) + low
                good = jnp.logical_and(row_at >= row_low, row_at < row_high)
                rows = slice(low, low + block)
                for plane in range(2):
                    for k in range(3):
                        value = acc[k, plane, rows]
                        kept = good
                        if k == 0:
                            value = value + rcol[e, 0, plane, rows]
                            kept = jnp.logical_and(good, lanes >= col_low)
                        elif k == 2:
                            value = value + rcol[e, 1, plane, rows]
                            kept = jnp.logical_and(good, lanes < col_high)
                        ext[k, plane, rows] += jnp.where(
                            kept, object_rate * value, jnp.zeros_like(value)
                        )
        else:
            spot = lax.broadcasted_iota(jnp.int32, (margin, LANES), 1) < margin
            for low in range(0, tile, margin):
                rows = slice(margin + low, 2 * margin + low)
                for plane in range(2):
                    turned = []
                    for k in range(3):
                        value = acc[k, plane, rows]
                        if k != 1:
                            value = value + rcol[e, k // 2, plane, rows]
                        value = ext[k, plane, rows] + object_rate * value
                        turned.append(pltpu.roll(value, margin, 1))
                    out_obj[plane, low : low + margin] = jnp.concatenate(
                        [jnp.where(spot, turned[k], turned[k + 1]) for k in range(2)], 1
                    )
        sent(e)
        if subset == SUBSETS - 1:
            sum_sent(outer_step)
            if not last:
                gather_end(g + 1)


def tiles(object_field, probe_modes, measured, positions, subset_order):
    n_row, n_col = lax.axis_size("row"), lax.axis_size("col")
    tile = object_field.shape[1]
    modes, pr, pw = probe_modes.shape
    pos_count, width = measured.shape[2], measured.shape[3]
    strip = 2 * MARGIN
    fits = (
        pos_count == SUBSETS and strip == LANES and width == 2 * LANES and tile == width
        and n_col % 2 == 0 and pw == LANES and pr % 8 == 0 and strip % pr == 0
        and n_row % 2 == 0
    )
    if not fits:
        return shards(object_field, probe_modes, measured, positions, subset_order)
    extent = tile + strip
    passes = OUTER * SUBSETS
    half = n_col // 2
    probe_rate = 0.5 / (pos_count * n_row * n_col)
    left_tables, right_forward, right_inverse = host_tables(width)
    f32, bf16 = jnp.float32, jnp.bfloat16
    vmem = pl.BlockSpec(memory_space=pltpu.VMEM)
    smem = pl.BlockSpec(memory_space=pltpu.SMEM)
    copies = (passes + 1) * 16 + 4 + 4 * OUTER * n_row * n_col
    far = pl.BlockSpec(memory_space=pltpu.HBM)
    return pl.pallas_call(
        functools.partial(kernel, n_row, n_col, probe_rate),
        out_shape=(
            jax.ShapeDtypeStruct(object_field.shape, f32),
            jax.ShapeDtypeStruct(probe_modes.shape, f32),
        ),
        in_specs=[smem, smem] + [far] * 6,
        out_specs=(vmem, vmem),
        scratch_shapes=[
            pltpu.VMEM((3, 2, extent, LANES), f32),
            pltpu.VMEM((3, 2, extent, LANES), f32),
            pltpu.VMEM((2, 2, width + 2 * strip, LANES), f32),
            pltpu.VMEM((2, width, width), f32),
            pltpu.VMEM((modes, width, 2 * width), f32),
            pltpu.VMEM((modes, width, 2 * width), bf16),
            pltpu.VMEM((modes, width, 2 * width), bf16),
            pltpu.VMEM((SUBSETS, 2, 8, LANES), jnp.int32),
            pltpu.VMEM((2, SUBSETS, 2, 8, LANES), jnp.int32),
            pltpu.VMEM((4, MARGIN, width), f32),
            pltpu.VMEM((2, 2, MARGIN, width), f32),
            pltpu.VMEM((passes, 4, MARGIN, width), f32),
            pltpu.VMEM((passes, 4, MARGIN, width), f32),
            pltpu.VMEM((passes + 1, 2, 2, extent, LANES), f32),
            pltpu.VMEM((OUTER, n_col, n_row, modes, pr, pw), f32),
            pltpu.VMEM((n_col, n_row, modes, pr, pw), f32),
            pltpu.VMEM((half, n_row, modes, pr, pw), f32),
            pltpu.VMEM((OUTER, half, n_row, modes, pr, pw), f32),
            pltpu.VMEM((OUTER, half, n_row, modes, pr, pw), f32),
            pltpu.VMEM((n_row // 2, modes, pr, pw), f32),
            pltpu.VMEM((OUTER, n_row // 2, modes, pr, pw), f32),
            pltpu.VMEM((n_row // 2, modes, pr, pw), f32),
            pltpu.VMEM((OUTER, n_row // 2, modes, pr, pw), f32),
            pltpu.VMEM(object_field.shape, f32),
            pltpu.VMEM((pos_count, width, width), f32),
            pltpu.VMEM(left_tables.shape, bf16),
            pltpu.VMEM(right_forward.shape, bf16),
            pltpu.VMEM(right_inverse.shape, bf16),
            pltpu.SemaphoreType.DMA((copies,)),
            pltpu.SemaphoreType.DMA((copies,)),
            pltpu.SemaphoreType.DMA((6,)),
        ],
        compiler_params=pltpu.CompilerParams(
            collective_id=0, has_side_effects=True, vmem_limit_bytes=48 * 1024 * 1024
        ),
    )(
        positions[0, 0], subset_order[0, 0], object_field, probe_modes, measured[0, 0],
        jnp.asarray(left_tables), jnp.asarray(right_forward), jnp.asarray(right_inverse),
    )


def solution(mesh):
    in_specs = (
        P(None, "row", "col"),
        P(None, "row", "col"),
        P("row", "col", None, None, None),
        P("row", "col", None, None),
        P("row", "col", None),
    )
    out_specs = (P(None, "row", "col"), P(None, "row", "col"))
    return jax.shard_map(tiles, mesh=mesh, in_specs=in_specs, out_specs=out_specs, check_vma=False)
```

```python
import functools
import math

import jax
import jax.numpy as jnp
import ml_dtypes
import numpy as np
from jax import lax
from jax.experimental import pallas as pl
from jax.experimental.pallas import tpu as pltpu
from jax.sharding import PartitionSpec as P

MARGIN = 64
SUBSETS = 2
OUTER = 2


amp_floor = 0.3
object_rate = 0.05


def extended_2(block, sides, width):
    for axis, dim in sides:
        count = lax.axis_size(axis)
        forward = [(i, i + 1) for i in range(count - 1)]
        backward = [(target, source) for source, target in forward]
        low = lax.ppermute(
            lax.slice_in_dim(block, block.shape[dim] - width, None, axis=dim), axis, forward
        )
        high = lax.ppermute(lax.slice_in_dim(block, 0, width, axis=dim), axis, backward)
        block = jnp.concatenate([low, block, high], axis=dim)
    return block


def tables(probe_size):
    ramp_values = jnp.arange(probe_size, dtype=jnp.int32)
    phases = ramp_values[:, None] * ramp_values[None, :] % probe_size
    angles = phases.astype(jnp.float32) * (2.0 * math.pi / probe_size)
    norming = 1.0 / math.sqrt(probe_size)
    cosine = jnp.cos(angles) * norming
    sine_part = jnp.sin(angles) * norming
    left_tables = jnp.stack([cosine, sine_part]).astype(jnp.bfloat16)
    right_forward = jnp.concatenate(
        [jnp.concatenate([cosine, -sine_part], 1), jnp.concatenate([sine_part, cosine], 1)], 0
    ).astype(jnp.bfloat16)
    right_inverse = jnp.concatenate(
        [jnp.concatenate([cosine, sine_part], 1), jnp.concatenate([-sine_part, cosine], 1)], 0
    ).astype(jnp.bfloat16)
    return (left_tables, right_forward, right_inverse)


def halves(values):
    middle = values.shape[-1] // 2
    return (values[..., :middle], values[..., middle:])


def multiply(former, latter, conjugate):
    former_re, former_im = halves(former)
    latter_re, latter_im = halves(latter)
    if conjugate:
        return jnp.concatenate(
            [
                former_re * latter_re + former_im * latter_im,
                former_re * latter_im - former_im * latter_re,
            ],
            -1,
        )
    return jnp.concatenate(
        [
            former_re * latter_re - former_im * latter_im,
            former_re * latter_im + former_im * latter_re,
        ],
        -1,
    )


def left_apply(left_tables, stacked, direction):
    products = jnp.einsum("tij,bjk->tbik", left_tables, stacked, preferred_element_type=jnp.float32)
    cos_re, cos_im = halves(products[0])
    sin_re, sin_im = halves(products[1])
    return jnp.concatenate([cos_re + direction * sin_im, cos_im - direction * sin_re], -1)


def project(windows, probe_full, amplitudes, left_tables, right_forward, right_inverse):
    exit_wave = multiply(probe_full[None], windows[:, None], False)
    count, mode_count, rows_here, cols_here = exit_wave.shape
    stacked = exit_wave.reshape(count * mode_count, rows_here, cols_here).astype(jnp.bfloat16)
    half_transform = left_apply(left_tables, stacked, 1.0).astype(jnp.bfloat16)
    far_field = jnp.einsum(
        "bik,kl->bil", half_transform, right_forward, preferred_element_type=jnp.float32
    )
    far_field = far_field.reshape(count, mode_count, rows_here, cols_here)
    far_re, far_im = halves(far_field)
    intensity = jnp.sum(far_re * far_re + far_im * far_im, axis=1)
    scaling = amplitudes / jnp.maximum(jnp.sqrt(intensity), amp_floor)
    scaling = jnp.concatenate([scaling, scaling], -1)[:, None]
    corrected = (
        (far_field * scaling).astype(jnp.bfloat16).reshape(count * mode_count, rows_here, cols_here)
    )
    returned = left_apply(left_tables, corrected, -1.0).astype(jnp.bfloat16)
    near_field = jnp.einsum(
        "bik,kl->bil", returned, right_inverse, preferred_element_type=jnp.float32
    )
    change = near_field.reshape(count, mode_count, rows_here, cols_here) - exit_wave
    window_gradient = jnp.sum(multiply(probe_full[None], change, True), axis=1)
    probe_gradient = jnp.sum(multiply(windows[:, None], change, True), axis=0)
    return (window_gradient, probe_gradient)


def spread(owned):
    gathered = lax.all_gather(owned, "col", axis=2, tiled=True)
    return lax.all_gather(gathered, "row", axis=1, tiled=True)


def fold(grad_extended, margin, tile_size):
    margins = jnp.concatenate(
        [grad_extended[:, :margin], grad_extended[:, tile_size + margin :]], 1
    )
    received = extended_2(margins, (("row", 1),), margin)
    interior = grad_extended[:, margin : margin + tile_size]
    interior = interior.at[:, :margin].add(received[:, :margin])
    interior = interior.at[:, tile_size - margin :].add(received[:, 3 * margin :])
    margins = jnp.concatenate([interior[:, :, :margin], interior[:, :, tile_size + margin :]], 2)
    received = extended_2(margins, (("col", 2),), margin)
    interior = interior[:, :, margin : margin + tile_size]
    interior = interior.at[:, :, :margin].add(received[:, :, :margin])
    interior = interior.at[:, :, tile_size - margin :].add(received[:, :, 3 * margin :])
    return interior


def shards(object_field, probe_modes, measured, positions, subset_order):
    probe_size = measured.shape[3]
    tile_size = object_field.shape[1]
    margin = MARGIN
    extent = tile_size + 2 * margin
    left_tables, right_forward, right_inverse = tables(probe_size)
    pos_count = subset_order.shape[2]
    subset_size = pos_count // SUBSETS
    probe_rate = 0.5 / (pos_count * lax.axis_size("row") * lax.axis_size("col"))
    probe_full = spread(probe_modes)
    for outer_step in range(OUTER):
        probe_total = jnp.zeros(probe_full.shape, jnp.float32)
        for subset in range(SUBSETS):
            extended = extended_2(object_field, (("row", 1), ("col", 2)), margin)
            chosen = subset_order[0, 0, subset * subset_size : (subset + 1) * subset_size]
            offsets = positions[0, 0][chosen]
            amplitudes = measured[0, 0][chosen]
            windows = []
            member = 0
            window_planes = lax.dynamic_slice(
                extended,
                (jnp.int32(0), offsets[member, 0], offsets[member, 1]),
                (2, probe_size, probe_size),
            )
            windows.append(jnp.concatenate([window_planes[0], window_planes[1]], -1))
            windows = jnp.stack(windows)
            window_gradient, probe_part = project(
                windows, probe_full, amplitudes, left_tables, right_forward, right_inverse
            )
            grad_extended = jnp.zeros((2, extent, extent), jnp.float32)
            member = 0
            grad_re, grad_im = halves(window_gradient[member])
            starts = (jnp.int32(0), offsets[member, 0], offsets[member, 1])
            grad_extended = lax.dynamic_update_slice(
                grad_extended, jnp.stack([grad_re, grad_im]), starts
            )
            object_field = object_field + object_rate * fold(grad_extended, margin, tile_size)
            probe_total = probe_total + probe_part
        owned_sum = lax.psum_scatter(probe_total, "row", scatter_dimension=1, tiled=True)
        owned_sum = lax.psum_scatter(owned_sum, "col", scatter_dimension=2, tiled=True)
        probe_modes = probe_modes + probe_rate * owned_sum
        if outer_step + 1 < OUTER:
            probe_full = spread(probe_modes)
    return (object_field, probe_modes)


LANES = 128


def host_tables(probe_size):
    ramp_values = np.arange(probe_size, dtype=np.int32)
    phases = ramp_values[:, None] * ramp_values[None, :] % probe_size
    angles = phases.astype(np.float32) * np.float32(2.0 * math.pi / probe_size)
    norming = np.float32(1.0 / math.sqrt(probe_size))
    cosine = np.cos(angles) * norming
    sine_part = np.sin(angles) * norming
    left_tables = np.stack([cosine, sine_part]).astype(ml_dtypes.bfloat16)
    right_forward = np.block([[cosine, -sine_part], [sine_part, cosine]]).astype(ml_dtypes.bfloat16)
    right_inverse = np.block([[cosine, sine_part], [-sine_part, cosine]]).astype(ml_dtypes.bfloat16)
    return (left_tables, right_forward, right_inverse)


def kernel(
    n_row, n_col, probe_rate,
    pos_ref, order_ref, obj_far, prb_ref, meas_far, lt_far, rf_far, ri_far,
    out_obj, out_prb,
    ext, acc, gpad, win, ew, xb, zb, offs, roffs, srow, rrow, rnear, rfar, rcol,
    pf, pg, hs, rc, ry, sx, rx, ss, rr,
    obj_ref, meas_ref, lt_ref, rf_ref, ri_ref, ssem, rsem, lsem,
):
    r = lax.axis_index("row")
    c = lax.axis_index("col")
    tile = obj_far.shape[1]
    width = meas_far.shape[1]
    modes, pr, pw = prb_ref.shape
    margin = MARGIN
    strip = 2 * margin
    extent = tile + strip
    passes = OUTER * SUBSETS
    half = n_col // 2
    core = lax.rem(c, 2)
    q = lax.div(c, 2)
    sibling = c + 1 - 2 * core
    block = strip
    blocks = width // block
    pieces = block // pr
    f32 = jnp.float32
    ids = {}

    def sem_id(key):
        return ids.setdefault(key, len(ids))

    def copy(key, src, dst, device):
        index = sem_id(key)
        return pltpu.make_async_remote_copy(
            src_ref=src, dst_ref=dst, send_sem=ssem.at[index], recv_sem=rsem.at[index],
            device_id=device, device_id_type=pl.DeviceIdType.MESH,
        )

    nz = n_row // 2
    z = lax.div(r, 2)
    odd = lax.rem(r, 2)
    pair = r + 1 - 2 * odd

    loads = [
        pltpu.make_async_copy(src, dst, lsem.at[index])
        for index, (src, dst) in enumerate(
            (
                (obj_far, obj_ref), (lt_far, lt_ref), (rf_far, rf_ref), (meas_far, meas_ref),
                (ri_far, ri_ref), (prb_ref, pf.at[0, c, r]),
            )
        )
    ]
    for load in loads:
        load.start()

    barrier = pltpu.get_barrier_semaphore()
    for step in range(1, n_row):
        pl.semaphore_signal(
            barrier, inc=1, device_id=(lax.rem(r + step, n_row), c),
            device_id_type=pl.DeviceIdType.MESH,
        )
    for step in range(1, n_col):
        pl.semaphore_signal(
            barrier, inc=1, device_id=(r, lax.rem(c + step, n_col)),
            device_id_type=pl.DeviceIdType.MESH,
        )
    pl.semaphore_wait(barrier, n_row - 1 + n_col - 1)

    has_up, has_down = r > 0, r < n_row - 1
    has_left, has_right = c > 0, c < n_col - 1
    lanes = lax.broadcasted_iota(jnp.int32, (block, LANES), 1)


    def row_copy(e, side):
        low = 0 if side == 0 else tile - margin
        src = obj_far.at[:, pl.ds(low, margin)]
        return copy(
            ("row", e, side), src, rrow.at[1 - side], (r - 1 if side == 0 else r + 1, c)
        )

    def chunks(e):
        return 2 if e == passes else 2 * (strip // margin)

    def near_copy(e, j):
        return copy(("near", e, j), srow.at[j], rnear.at[e - 1, j], (pair, c))

    def far_copy(e, j):
        to = jnp.where(odd == 1, r - 2, r + 2)
        return copy(("far", e, j), rnear.at[e - 1, j], rfar.at[e - 1, j], (to, c))

    even = odd == 0
    takes_far = jnp.logical_or(
        jnp.logical_and(even, has_up), jnp.logical_and(jnp.logical_not(even), has_down)
    )
    gives_far = jnp.logical_or(
        jnp.logical_and(even, r < n_row - 2), jnp.logical_and(jnp.logical_not(even), r > 1)
    )

    def strip_low(e, part):
        top = margin if e == passes else 0
        if part == 0:
            return pl.multiple_of(jnp.where(even, tile, top), margin)
        return pl.multiple_of(jnp.where(even, top, tile), margin)

    def col_copy(e, side, part):
        if part == 1:
            low, size = strip, tile - strip
        elif e == 0:
            low, size = (0, tile)[part // 2], strip
        else:
            low, size = strip_low(e, part), margin if e == passes else strip
        rows = pl.ds(low, size)
        src = acc.at[2 * side, :, rows]
        dst = rcol.at[e, 1 - side, :, rows]
        return copy(("col", e, side, part), src, dst, (r, c - 1 if side == 0 else c + 1))

    def off_copy(side):
        return copy(("off", side), offs, roffs.at[1 - side], (r - 1 if side == 0 else r + 1, c))

    def start_cols(e, part):
        @pl.when(has_left)
        def _():
            col_copy(e, 0, part).start()

        @pl.when(has_right)
        def _():
            col_copy(e, 1, part).start()


    def piece_at(step, other_half, sign):
        place = 2 * lax.rem(z + (step if sign > 0 else nz - step), nz)
        return place + (1 - odd if other_half else odd)

    def own_or(g, held, step, other_half):
        if g == 0 and step == 0 and other_half == 0:
            return prb_ref
        return pf.at[g, held, piece_at(step, other_half, -1)]

    def ag_z(g, step):
        to = 2 * lax.rem(z + step, nz) + odd
        return copy(("agz", g, step), own_or(g, c, 0, 0), pf.at[g, c, r], (to, c))

    def ag_x(g, step):
        at = piece_at(step, 0, -1)
        return copy(("agx", g, step), own_or(g, c, step, 0), pf.at[g, c, at], (pair, c))

    def ag_sib(g, step, s):
        at = piece_at(step, s, -1)
        return copy(("ags", g, step, s), own_or(g, c, step, s), pf.at[g, c, at], (r, sibling))

    def ag_par(g, step, s, other):
        at = piece_at(step, s, -1)
        to = 2 * lax.rem(q + other, half) + core
        return copy(("agp", g, step, s, other), own_or(g, c, step, s), pf.at[g, c, at], (r, to))

    def ag_fwd(g, step, s, other):
        at = piece_at(step, s, -1)
        held = 2 * lax.rem(q + half - other, half) + core
        return copy(
            ("agf", g, step, s, other), pf.at[g, held, at], pf.at[g, held, at], (r, sibling)
        )

    def hand_on(g, step, s):
        for other in range(1, half):
            ag_par(g, step, s, other).start()
        ag_sib(g, step, s).start()

    def gather_send(g):
        for step in range(1, nz):
            ag_z(g, step).start()
        ag_x(g, 0).start()
        hand_on(g, 0, 0)

    def gather_first(g):
        for step in range(1, nz):
            ag_z(g, step).wait_recv()
            ag_x(g, step).start()
            hand_on(g, step, 0)

    def gather_second(g):
        for step in range(nz):
            ag_x(g, step).wait_recv()
            hand_on(g, step, 1)

    def gather_third(g):
        for s in range(2):
            for step in range(nz):
                for other in range(1, half):
                    ag_par(g, step, s, other).wait_recv()
                    ag_fwd(g, step, s, other).start()

    def gather_end(g):
        for s in range(2):
            for step in range(nz):
                ag_sib(g, step, s).wait_recv()
                for other in range(1, half):
                    ag_fwd(g, step, s, other).wait_recv()
        for step in range(nz):
            if step:
                ag_z(g, step).wait_send()
            ag_x(g, step).wait_send()
            for s in range(2):
                ag_sib(g, step, s).wait_send()
                for other in range(1, half):
                    ag_par(g, step, s, other).wait_send()
                    ag_fwd(g, step, s, other).wait_send()


    def rs_core(t, k, i):
        at = pl.ds(i * pieces, pieces)
        return copy(
            ("rsc", t, k, i), pg.at[2 * k + 1 - core, at], rc.at[t, k, at], (r, sibling)
        )

    def rs_par(t, step, s, other):
        at = piece_at(step, s, 1)
        to_q = lax.rem(q + other, half)
        return copy(
            ("rsp", t, step, s, other), hs.at[to_q, at], ry.at[t, other, at],
            (r, 2 * to_q + core),
        )

    def rs_x(t, step):
        return copy(("rsx", t, step), sx.at[step], rx.at[t, step], (pair, c))

    def rs_z(t, step):
        to = 2 * lax.rem(z + step, nz) + odd
        return copy(("rsz", t, step), ss.at[step], rr.at[t, step], (to, c))

    def sum_start(t, i):
        for k in range(half):
            rs_core(t, k, i).start()

    order = list(range(1, nz)) + [0]

    def sum_pass_on(t):
        for i in range(blocks):
            for k in range(half):
                rs_core(t, k, i).wait_recv()
        for s in (1, 0):
            for step in order:
                at = piece_at(step, s, 1)
                for other in range(1, half):
                    to_q = lax.rem(q + other, half)
                    hs[to_q, at] = pg[2 * to_q + core, at] + rc[t, to_q, at]
                    rs_par(t, step, s, other).start()

    def sum_piece(t, step, s):
        at = piece_at(step, s, 1)
        value = pg[c, at] + rc[t, q, at]
        for other in range(1, half):
            rs_par(t, step, s, other).wait_recv()
            value = value + ry[t, other, at]
        return value

    def sum_far(t):
        for step in order:
            sx[step] = sum_piece(t, step, 1)
            rs_x(t, step).start()

    def sum_near(t):
        for step in order:
            value = sum_piece(t, step, 0)
            rs_x(t, step).wait_recv()
            ss[step] = value + rx[t, step]
            if step:
                rs_z(t, step).start()

    def sum_end(t):
        value = ss[0]
        for step in range(1, nz):
            rs_z(t, step).wait_recv()
            value = value + rr[t, step]
        return value

    def sum_sent(t):
        for i in range(blocks):
            for k in range(half):
                rs_core(t, k, i).wait_send()
        for step in range(nz):
            for s in range(2):
                for other in range(1, half):
                    rs_par(t, step, s, other).wait_send()
            rs_x(t, step).wait_send()
            if step:
                rs_z(t, step).wait_send()


    for subset in range(SUBSETS):
        for d in range(2):
            offs[subset, d] = jnp.full(
                offs.shape[2:], pos_ref[order_ref[subset], d], jnp.int32
            )

    @pl.when(has_up)
    def _():
        row_copy(0, 0).start()
        off_copy(0).start()

    @pl.when(has_down)
    def _():
        row_copy(0, 1).start()
        off_copy(1).start()

    gather_send(0)
    loads[0].wait()

    def placed(values):
        rows = values.shape[0]
        spot = lax.broadcasted_iota(jnp.int32, (rows, LANES), 1) >= margin
        first = pltpu.roll(values[:, :LANES], margin, 1)
        second = pltpu.roll(values[:, LANES:], margin, 1)
        zero = jnp.zeros_like(first)
        return (
            jnp.where(spot, first, zero), jnp.where(spot, second, first),
            jnp.where(spot, zero, second),
        )

    for plane in range(2):
        for k in range(2):
            gpad[plane, k, 0:strip] = jnp.zeros((strip, LANES), f32)
            gpad[plane, k, strip + width :] = jnp.zeros((strip, LANES), f32)
        for low in range(0, tile, margin):
            parts = placed(obj_ref[plane, low : low + margin])
            for b in range(3):
                acc[b, plane, margin + low : 2 * margin + low] = parts[b]
    start_cols(0, 1)
    gather_first(0)

    def halo_rows(side, at):
        for plane in range(2):
            parts = placed(rrow[side, plane])
            for b in range(3):
                acc[b, plane, at : at + margin] = parts[b]

    def halo_zero(at):
        for plane in range(2):
            for b in range(3):
                acc[b, plane, at : at + margin] = jnp.zeros((margin, LANES), f32)

    @pl.when(has_down)
    def _():
        row_copy(0, 0).wait_recv()
        off_copy(0).wait_recv()
        halo_rows(1, tile + margin)

    @pl.when(jnp.logical_not(has_down))
    def _():
        halo_zero(tile + margin)

    start_cols(0, 2)
    gather_second(0)

    @pl.when(has_up)
    def _():
        row_copy(0, 1).wait_recv()
        off_copy(1).wait_recv()
        halo_rows(0, 0)

    @pl.when(jnp.logical_not(has_up))
    def _():
        halo_zero(0)

    start_cols(0, 0)
    gather_third(0)

    def take_cols(e):
        for part in range(3):
            @pl.when(has_left)
            def _():
                col_copy(e, 1, part).wait_recv()

            @pl.when(has_right)
            def _():
                col_copy(e, 0, part).wait_recv()

    def sent(e):
        if e == 0:
            @pl.when(has_up)
            def _():
                row_copy(e, 0).wait_send()

            @pl.when(has_down)
            def _():
                row_copy(e, 1).wait_send()
        else:
            for j in range(chunks(e)):
                near_copy(e, j).wait_send()

            @pl.when(gives_far)
            def _():
                for j in range(chunks(e)):
                    far_copy(e, j).wait_send()

        for part in range(3):
            @pl.when(has_left)
            def _():
                col_copy(e, 0, part).wait_send()

            @pl.when(has_right)
            def _():
                col_copy(e, 1, part).wait_send()

    for side, there in ((0, has_left), (1, has_right)):
        @pl.when(jnp.logical_not(there))
        def _():
            for e in range(passes + 1):
                rcol[e, side] = jnp.zeros(rcol.shape[2:], f32)

    take_cols(0)
    for plane in range(2):
        ext[0, plane] = acc[0, plane] + rcol[0, 0, plane]
        ext[1, plane] = acc[1, plane]
        ext[2, plane] = acc[2, plane] + rcol[0, 1, plane]
    sent(0)

    @pl.when(has_up)
    def _():
        off_copy(0).wait_send()

    @pl.when(has_down)
    def _():
        off_copy(1).wait_send()

    gather_end(0)
    for load in loads[1:]:
        load.wait()

    def probe_block(g, m, i):
        parts = [
            pf[g, k, pl.ds(i * pieces, pieces), m].reshape(block, pw) for k in range(n_col)
        ]
        return (
            jnp.concatenate(parts[:half], 1), jnp.concatenate(parts[half:], 1)
        )

    def gradient_rows(plane, low, size):
        return jnp.concatenate([gpad[plane, k, pl.ds(low, size), :] for k in range(2)], 1)

    def unpacked(mask, values):
        zero = jnp.zeros_like(values[:, :LANES])
        return (
            jnp.where(mask, values[:, :LANES], zero), values[:, LANES:],
            jnp.where(mask, zero, values[:, :LANES]),
        )

    row_low = jnp.where(has_up, 0, margin)
    row_high = jnp.where(has_down, extent, extent - margin)
    col_low = jnp.where(has_left, 0, margin)
    col_high = jnp.where(has_right, LANES, margin)

    for number in range(passes):
        outer_step, subset = number // SUBSETS, number % SUBSETS
        g = outer_step
        e = number + 1
        last = e == passes
        chosen = order_ref[subset]
        a = pos_ref[chosen, 0]
        b = pos_ref[chosen, 1]
        back = lax.rem(LANES - b, LANES)
        ahead = lax.rem(b, LANES)

        @pl.loop(0, blocks)
        def _(i):
            rows = pl.ds(pl.multiple_of(i * block, block), block)
            planes = []
            for plane in range(2):
                turned = [
                    pltpu.roll(ext[k, plane, pl.ds(a + i * block, block), :], back, 1)
                    for k in range(3)
                ]
                inside = lanes < LANES - b
                window = jnp.concatenate(
                    [jnp.where(inside, turned[k], turned[k + 1]) for k in range(2)], 1
                )
                win[plane, rows] = window
                planes.append(window)
            for m in range(modes):
                p_re, p_im = probe_block(g, m, i)
                wave = jnp.concatenate(
                    [p_re * planes[0] - p_im * planes[1], p_re * planes[1] + p_im * planes[0]], 1
                )
                ew[m, rows] = wave
                xb[m, rows] = wave.astype(jnp.bfloat16)

        def transform(source, m, rows, direction, table_ref):
            cos = jnp.dot(lt_ref[0, rows], source[m], preferred_element_type=f32)
            sin = jnp.dot(lt_ref[1, rows], source[m], preferred_element_type=f32)
            mixed = jnp.concatenate(
                [
                    cos[:, :width] + direction * sin[:, width:],
                    cos[:, width:] - direction * sin[:, :width],
                ],
                1,
            ).astype(jnp.bfloat16)
            return jnp.dot(mixed, table_ref[...], preferred_element_type=f32)

        @pl.loop(0, blocks)
        def _(i):
            rows = pl.ds(pl.multiple_of(i * block, block), block)
            far = [transform(xb, m, rows, 1.0, rf_ref) for m in range(modes)]
            intensity = sum(
                f[:, :width] * f[:, :width] + f[:, width:] * f[:, width:] for f in far
            )
            scaling = meas_ref[chosen, rows] * jnp.minimum(
                lax.rsqrt(intensity), 1.0 / amp_floor
            )
            scaling = jnp.concatenate([scaling, scaling], 1)
            for m in range(modes):
                zb[m, rows] = (far[m] * scaling).astype(jnp.bfloat16)

        mask = lanes >= b
        for i in range(blocks):
            rows = slice(i * block, (i + 1) * block)
            w_re, w_im = win[0, rows], win[1, rows]
            g_re = g_im = None
            for m in range(modes):
                change = transform(zb, m, rows, -1.0, ri_ref) - ew[m, rows]
                c_re, c_im = change[:, :width], change[:, width:]
                p_re, p_im = probe_block(g, m, i)
                part_re, part_im = p_re * c_re + p_im * c_im, p_re * c_im - p_im * c_re
                g_re = part_re if m == 0 else g_re + part_re
                g_im = part_im if m == 0 else g_im + part_im
                grad = jnp.concatenate(
                    [w_re * c_re + w_im * c_im, w_re * c_im - w_im * c_re], 1
                )
                at = slice(i * pieces, (i + 1) * pieces)
                for k in range(n_col):
                    value = grad[:, k * pw : (k + 1) * pw].reshape(pieces, pr, pw)
                    if subset:
                        value = value + pg[k, at, m]
                    pg[k, at, m] = value
            for plane, values in enumerate((g_re, g_im)):
                first = pltpu.roll(values[:, :LANES], ahead, 1)
                second = pltpu.roll(values[:, LANES:], ahead, 1)
                at = slice(strip + i * block, strip + (i + 1) * block)
                gpad[plane, 0, at] = jnp.where(mask, first, second)
                gpad[plane, 1, at] = jnp.where(mask, second, first)
            if subset == SUBSETS - 1:
                sum_start(outer_step, i)

        for j in range(chunks(e)):
            if last:
                plane, top, bottom = j, 0, extent - margin
            else:
                plane, top = j // 2, j % 2 * margin
                bottom = tile + top
            srow[j] = gradient_rows(plane, strip + top - a, margin) + gradient_rows(
                plane, strip + bottom - a, margin
            )
            near_copy(e, j).start()

        if subset == SUBSETS - 1:
            sum_pass_on(outer_step)

        for low in (strip, 0, tile):
            for plane in range(2):
                parts = unpacked(mask, gradient_rows(plane, strip + low - a, strip))
                for k in range(3):
                    acc[k, plane, low : low + strip] = parts[k]
            if low == strip:
                start_cols(e, 1)

        def add_rows(part, take, arrived):
            from_down = even if part == 0 else jnp.logical_not(even)
            side = jnp.where(from_down, 1, 0)
            low = strip_low(e, part)
            there_a, there_b = roffs[side, subset, 0, 0:1, :], roffs[side, subset, 1, 0:1, :]
            spot = lax.broadcasted_iota(jnp.int32, (margin, LANES), 1) >= there_b
            row_at = lax.broadcasted_iota(jnp.int32, (margin, LANES), 0)
            for j in range(chunks(e)):
                take(e, j).wait_recv()
                plane, top = (j, 0) if last else (j // 2, j % 2 * margin)
                under = row_at + (margin if last else top)
                kept = jnp.where(from_down, row_at + top - there_a, there_a - 1 - under) >= 0
                values = arrived[e - 1, j]
                values = jnp.where(
                    jnp.concatenate([kept, kept], 1), values, jnp.zeros_like(values)
                )
                parts = unpacked(spot, values)
                rows = pl.ds(pl.multiple_of(low + top, margin), margin)
                for k in range(3):
                    acc[k, plane, rows] += parts[k]
                if part == 0:
                    @pl.when(gives_far)
                    def _():
                        far_copy(e, j).start()

        if subset == SUBSETS - 1:
            sum_far(outer_step)
        add_rows(0, near_copy, rnear)
        start_cols(e, 0)
        if subset == SUBSETS - 1:
            sum_near(outer_step)

        @pl.when(takes_far)
        def _():
            add_rows(2, far_copy, rfar)

        start_cols(e, 2)

        if subset == SUBSETS - 1:
            total = sum_end(outer_step)
            piece = pf[g, c, r] + probe_rate * total
            if last:
                out_prb[...] = piece
            else:
                pf[g + 1, c, r] = piece
                gather_send(g + 1)
                gather_first(g + 1)
                gather_second(g + 1)
                gather_third(g + 1)

        take_cols(e)
        if not last:
            for low in range(0, extent, block):
                row_at = lax.broadcasted_iota(jnp.int32, (block, LANES), 0) + low
                good = jnp.logical_and(row_at >= row_low, row_at < row_high)
                rows = slice(low, low + block)
                for plane in range(2):
                    for k in range(3):
                        value = acc[k, plane, rows]
                        kept = good
                        if k == 0:
                            value = value + rcol[e, 0, plane, rows]
                            kept = jnp.logical_and(good, lanes >= col_low)
                        elif k == 2:
                            value = value + rcol[e, 1, plane, rows]
                            kept = jnp.logical_and(good, lanes < col_high)
                        ext[k, plane, rows] += jnp.where(
                            kept, object_rate * value, jnp.zeros_like(value)
                        )
        else:
            spot = lax.broadcasted_iota(jnp.int32, (margin, LANES), 1) < margin
            for low in range(0, tile, margin):
                rows = slice(margin + low, 2 * margin + low)
                for plane in range(2):
                    turned = []
                    for k in range(3):
                        value = acc[k, plane, rows]
                        if k != 1:
                            value = value + rcol[e, k // 2, plane, rows]
                        value = ext[k, plane, rows] + object_rate * value
                        turned.append(pltpu.roll(value, margin, 1))
                    out_obj[plane, low : low + margin] = jnp.concatenate(
                        [jnp.where(spot, turned[k], turned[k + 1]) for k in range(2)], 1
                    )
        sent(e)
        if subset == SUBSETS - 1:
            sum_sent(outer_step)
            if not last:
                gather_end(g + 1)


def tiles(object_field, probe_modes, measured, positions, subset_order):
    n_row, n_col = lax.axis_size("row"), lax.axis_size("col")
    tile = object_field.shape[1]
    modes, pr, pw = probe_modes.shape
    pos_count, width = measured.shape[2], measured.shape[3]
    strip = 2 * MARGIN
    fits = (
        pos_count == SUBSETS and strip == LANES and width == 2 * LANES and tile == width
        and n_col % 2 == 0 and pw == LANES and pr % 8 == 0 and strip % pr == 0
        and n_row % 2 == 0
    )
    if not fits:
        return shards(object_field, probe_modes, measured, positions, subset_order)
    extent = tile + strip
    passes = OUTER * SUBSETS
    half = n_col // 2
    probe_rate = 0.5 / (pos_count * n_row * n_col)
    left_tables, right_forward, right_inverse = host_tables(width)
    f32, bf16 = jnp.float32, jnp.bfloat16
    vmem = pl.BlockSpec(memory_space=pltpu.VMEM)
    smem = pl.BlockSpec(memory_space=pltpu.SMEM)
    copies = (passes + 1) * 16 + 4 + 4 * OUTER * n_row * n_col
    far = pl.BlockSpec(memory_space=pltpu.HBM)
    return pl.pallas_call(
        functools.partial(kernel, n_row, n_col, probe_rate),
        out_shape=(
            jax.ShapeDtypeStruct(object_field.shape, f32),
            jax.ShapeDtypeStruct(probe_modes.shape, f32),
        ),
        in_specs=[smem, smem] + [far] * 6,
        out_specs=(vmem, vmem),
        scratch_shapes=[
            pltpu.VMEM((3, 2, extent, LANES), f32),
            pltpu.VMEM((3, 2, extent, LANES), f32),
            pltpu.VMEM((2, 2, width + 2 * strip, LANES), f32),
            pltpu.VMEM((2, width, width), f32),
            pltpu.VMEM((modes, width, 2 * width), f32),
            pltpu.VMEM((modes, width, 2 * width), bf16),
            pltpu.VMEM((modes, width, 2 * width), bf16),
            pltpu.VMEM((SUBSETS, 2, 8, LANES), jnp.int32),
            pltpu.VMEM((2, SUBSETS, 2, 8, LANES), jnp.int32),
            pltpu.VMEM((4, MARGIN, width), f32),
            pltpu.VMEM((2, 2, MARGIN, width), f32),
            pltpu.VMEM((passes, 4, MARGIN, width), f32),
            pltpu.VMEM((passes, 4, MARGIN, width), f32),
            pltpu.VMEM((passes + 1, 2, 2, extent, LANES), f32),
            pltpu.VMEM((OUTER, n_col, n_row, modes, pr, pw), f32),
            pltpu.VMEM((n_col, n_row, modes, pr, pw), f32),
            pltpu.VMEM((half, n_row, modes, pr, pw), f32),
            pltpu.VMEM((OUTER, half, n_row, modes, pr, pw), f32),
            pltpu.VMEM((OUTER, half, n_row, modes, pr, pw), f32),
            pltpu.VMEM((n_row // 2, modes, pr, pw), f32),
            pltpu.VMEM((OUTER, n_row // 2, modes, pr, pw), f32),
            pltpu.VMEM((n_row // 2, modes, pr, pw), f32),
            pltpu.VMEM((OUTER, n_row // 2, modes, pr, pw), f32),
            pltpu.VMEM(object_field.shape, f32),
            pltpu.VMEM((pos_count, width, width), f32),
            pltpu.VMEM(left_tables.shape, bf16),
            pltpu.VMEM(right_forward.shape, bf16),
            pltpu.VMEM(right_inverse.shape, bf16),
            pltpu.SemaphoreType.DMA((copies,)),
            pltpu.SemaphoreType.DMA((copies,)),
            pltpu.SemaphoreType.DMA((6,)),
        ],
        compiler_params=pltpu.CompilerParams(
            collective_id=0, has_side_effects=True, vmem_limit_bytes=63 * 1024 * 1024 + 512 * 1024
        ),
    )(
        positions[0, 0], subset_order[0, 0], object_field, probe_modes, measured[0, 0],
        jnp.asarray(left_tables), jnp.asarray(right_forward), jnp.asarray(right_inverse),
    )


def solution(mesh):
    in_specs = (
        P(None, "row", "col"),
        P(None, "row", "col"),
        P("row", "col", None, None, None),
        P("row", "col", None, None),
        P("row", "col", None),
    )
    out_specs = (P(None, "row", "col"), P(None, "row", "col"))
    return jax.shard_map(tiles, mesh=mesh, in_specs=in_specs, out_specs=out_specs, check_vma=False)
```

```python
import functools
import math

import jax
import jax.numpy as jnp
import ml_dtypes
import numpy as np
from jax import lax
from jax.experimental import pallas as pl
from jax.experimental.pallas import tpu as pltpu
from jax.sharding import PartitionSpec as P

MARGIN = 64
SUBSETS = 2
OUTER = 2


amp_floor = 0.3
object_rate = 0.05


def extended_2(block, sides, width):
    for axis, dim in sides:
        count = lax.axis_size(axis)
        forward = [(i, i + 1) for i in range(count - 1)]
        backward = [(target, source) for source, target in forward]
        low = lax.ppermute(
            lax.slice_in_dim(block, block.shape[dim] - width, None, axis=dim), axis, forward
        )
        high = lax.ppermute(lax.slice_in_dim(block, 0, width, axis=dim), axis, backward)
        block = jnp.concatenate([low, block, high], axis=dim)
    return block


def tables(probe_size):
    ramp_values = jnp.arange(probe_size, dtype=jnp.int32)
    phases = ramp_values[:, None] * ramp_values[None, :] % probe_size
    angles = phases.astype(jnp.float32) * (2.0 * math.pi / probe_size)
    norming = 1.0 / math.sqrt(probe_size)
    cosine = jnp.cos(angles) * norming
    sine_part = jnp.sin(angles) * norming
    left_tables = jnp.stack([cosine, sine_part]).astype(jnp.bfloat16)
    right_forward = jnp.concatenate(
        [jnp.concatenate([cosine, -sine_part], 1), jnp.concatenate([sine_part, cosine], 1)], 0
    ).astype(jnp.bfloat16)
    right_inverse = jnp.concatenate(
        [jnp.concatenate([cosine, sine_part], 1), jnp.concatenate([-sine_part, cosine], 1)], 0
    ).astype(jnp.bfloat16)
    return (left_tables, right_forward, right_inverse)


def halves(values):
    middle = values.shape[-1] // 2
    return (values[..., :middle], values[..., middle:])


def multiply(former, latter, conjugate):
    former_re, former_im = halves(former)
    latter_re, latter_im = halves(latter)
    if conjugate:
        return jnp.concatenate(
            [
                former_re * latter_re + former_im * latter_im,
                former_re * latter_im - former_im * latter_re,
            ],
            -1,
        )
    return jnp.concatenate(
        [
            former_re * latter_re - former_im * latter_im,
            former_re * latter_im + former_im * latter_re,
        ],
        -1,
    )


def left_apply(left_tables, stacked, direction):
    products = jnp.einsum("tij,bjk->tbik", left_tables, stacked, preferred_element_type=jnp.float32)
    cos_re, cos_im = halves(products[0])
    sin_re, sin_im = halves(products[1])
    return jnp.concatenate([cos_re + direction * sin_im, cos_im - direction * sin_re], -1)


def project(windows, probe_full, amplitudes, left_tables, right_forward, right_inverse):
    exit_wave = multiply(probe_full[None], windows[:, None], False)
    count, mode_count, rows_here, cols_here = exit_wave.shape
    stacked = exit_wave.reshape(count * mode_count, rows_here, cols_here).astype(jnp.bfloat16)
    half_transform = left_apply(left_tables, stacked, 1.0).astype(jnp.bfloat16)
    far_field = jnp.einsum(
        "bik,kl->bil", half_transform, right_forward, preferred_element_type=jnp.float32
    )
    far_field = far_field.reshape(count, mode_count, rows_here, cols_here)
    far_re, far_im = halves(far_field)
    intensity = jnp.sum(far_re * far_re + far_im * far_im, axis=1)
    scaling = amplitudes / jnp.maximum(jnp.sqrt(intensity), amp_floor)
    scaling = jnp.concatenate([scaling, scaling], -1)[:, None]
    corrected = (
        (far_field * scaling).astype(jnp.bfloat16).reshape(count * mode_count, rows_here, cols_here)
    )
    returned = left_apply(left_tables, corrected, -1.0).astype(jnp.bfloat16)
    near_field = jnp.einsum(
        "bik,kl->bil", returned, right_inverse, preferred_element_type=jnp.float32
    )
    change = near_field.reshape(count, mode_count, rows_here, cols_here) - exit_wave
    window_gradient = jnp.sum(multiply(probe_full[None], change, True), axis=1)
    probe_gradient = jnp.sum(multiply(windows[:, None], change, True), axis=0)
    return (window_gradient, probe_gradient)


def spread(owned):
    gathered = lax.all_gather(owned, "col", axis=2, tiled=True)
    return lax.all_gather(gathered, "row", axis=1, tiled=True)


def fold(grad_extended, margin, tile_size):
    margins = jnp.concatenate(
        [grad_extended[:, :margin], grad_extended[:, tile_size + margin :]], 1
    )
    received = extended_2(margins, (("row", 1),), margin)
    interior = grad_extended[:, margin : margin + tile_size]
    interior = interior.at[:, :margin].add(received[:, :margin])
    interior = interior.at[:, tile_size - margin :].add(received[:, 3 * margin :])
    margins = jnp.concatenate([interior[:, :, :margin], interior[:, :, tile_size + margin :]], 2)
    received = extended_2(margins, (("col", 2),), margin)
    interior = interior[:, :, margin : margin + tile_size]
    interior = interior.at[:, :, :margin].add(received[:, :, :margin])
    interior = interior.at[:, :, tile_size - margin :].add(received[:, :, 3 * margin :])
    return interior


def shards(object_field, probe_modes, measured, positions, subset_order):
    probe_size = measured.shape[3]
    tile_size = object_field.shape[1]
    margin = MARGIN
    extent = tile_size + 2 * margin
    left_tables, right_forward, right_inverse = tables(probe_size)
    pos_count = subset_order.shape[2]
    subset_size = pos_count // SUBSETS
    probe_rate = 0.5 / (pos_count * lax.axis_size("row") * lax.axis_size("col"))
    probe_full = spread(probe_modes)
    for outer_step in range(OUTER):
        probe_total = jnp.zeros(probe_full.shape, jnp.float32)
        for subset in range(SUBSETS):
            extended = extended_2(object_field, (("row", 1), ("col", 2)), margin)
            chosen = subset_order[0, 0, subset * subset_size : (subset + 1) * subset_size]
            offsets = positions[0, 0][chosen]
            amplitudes = measured[0, 0][chosen]
            windows = []
            member = 0
            window_planes = lax.dynamic_slice(
                extended,
                (jnp.int32(0), offsets[member, 0], offsets[member, 1]),
                (2, probe_size, probe_size),
            )
            windows.append(jnp.concatenate([window_planes[0], window_planes[1]], -1))
            windows = jnp.stack(windows)
            window_gradient, probe_part = project(
                windows, probe_full, amplitudes, left_tables, right_forward, right_inverse
            )
            grad_extended = jnp.zeros((2, extent, extent), jnp.float32)
            member = 0
            grad_re, grad_im = halves(window_gradient[member])
            starts = (jnp.int32(0), offsets[member, 0], offsets[member, 1])
            grad_extended = lax.dynamic_update_slice(
                grad_extended, jnp.stack([grad_re, grad_im]), starts
            )
            object_field = object_field + object_rate * fold(grad_extended, margin, tile_size)
            probe_total = probe_total + probe_part
        owned_sum = lax.psum_scatter(probe_total, "row", scatter_dimension=1, tiled=True)
        owned_sum = lax.psum_scatter(owned_sum, "col", scatter_dimension=2, tiled=True)
        probe_modes = probe_modes + probe_rate * owned_sum
        if outer_step + 1 < OUTER:
            probe_full = spread(probe_modes)
    return (object_field, probe_modes)


LANES = 128


def host_tables(probe_size):
    ramp_values = np.arange(probe_size, dtype=np.int32)
    phases = ramp_values[:, None] * ramp_values[None, :] % probe_size
    angles = phases.astype(np.float32) * np.float32(2.0 * math.pi / probe_size)
    norming = np.float32(1.0 / math.sqrt(probe_size))
    cosine = np.cos(angles) * norming
    sine_part = np.sin(angles) * norming
    left_tables = np.stack([cosine, sine_part]).astype(ml_dtypes.bfloat16)
    right_forward = np.block([[cosine, -sine_part], [sine_part, cosine]]).astype(ml_dtypes.bfloat16)
    right_inverse = np.block([[cosine, sine_part], [-sine_part, cosine]]).astype(ml_dtypes.bfloat16)
    return (left_tables, right_forward, right_inverse)


def kernel(
    n_row, n_col, probe_rate,
    pos_ref, order_ref, obj_far, prb_ref, meas_far, lt_far, rf_far, ri_far,
    out_obj, out_prb,
    ext, acc, gpad, win, ew, xb, zb, offs, roffs, srow, rrow, rnear, rfar, rcol,
    pf, pg, hs, rc, ry, sx, rx, ss, rr,
    obj_ref, meas_ref, lt_ref, rf_ref, ri_ref, ssem, rsem, lsem,
):
    r = lax.axis_index("row")
    c = lax.axis_index("col")
    tile = obj_far.shape[1]
    width = meas_far.shape[1]
    modes, pr, pw = prb_ref.shape
    margin = MARGIN
    strip = 2 * margin
    extent = tile + strip
    passes = OUTER * SUBSETS
    half = n_col // 2
    core = lax.rem(c, 2)
    q = lax.div(c, 2)
    sibling = c + 1 - 2 * core
    block = strip
    blocks = width // block
    pieces = block // pr
    f32 = jnp.float32
    ids = {}

    def sem_id(key):
        return ids.setdefault(key, len(ids))

    def copy(key, src, dst, device):
        index = sem_id(key)
        return pltpu.make_async_remote_copy(
            src_ref=src, dst_ref=dst, send_sem=ssem.at[index], recv_sem=rsem.at[index],
            device_id=device, device_id_type=pl.DeviceIdType.MESH,
        )

    nz = n_row // 2
    z = lax.div(r, 2)
    odd = lax.rem(r, 2)
    pair = r + 1 - 2 * odd

    loads = [
        pltpu.make_async_copy(src, dst, lsem.at[index])
        for index, (src, dst) in enumerate(
            (
                (obj_far, obj_ref), (lt_far, lt_ref), (rf_far, rf_ref), (meas_far, meas_ref),
                (ri_far, ri_ref), (prb_ref, pf.at[0, c, r]),
            )
        )
    ]
    for load in loads:
        load.start()

    barrier = pltpu.get_barrier_semaphore()
    for step in range(1, n_row):
        pl.semaphore_signal(
            barrier, inc=1, device_id=(lax.rem(r + step, n_row), c),
            device_id_type=pl.DeviceIdType.MESH,
        )
    for step in range(1, n_col):
        pl.semaphore_signal(
            barrier, inc=1, device_id=(r, lax.rem(c + step, n_col)),
            device_id_type=pl.DeviceIdType.MESH,
        )
    pl.semaphore_wait(barrier, n_row - 1 + n_col - 1)

    has_up, has_down = r > 0, r < n_row - 1
    has_left, has_right = c > 0, c < n_col - 1
    lanes = lax.broadcasted_iota(jnp.int32, (block, LANES), 1)


    def row_copy(e, side):
        low = 0 if side == 0 else tile - margin
        src = obj_far.at[:, pl.ds(low, margin)]
        return copy(
            ("row", e, side), src, rrow.at[1 - side], (r - 1 if side == 0 else r + 1, c)
        )

    def chunks(e):
        return 2 if e == passes else 2 * (strip // margin)

    def near_copy(e, j):
        return copy(("near", e, j), srow.at[j], rnear.at[e - 1, j], (pair, c))

    def far_copy(e, j):
        to = jnp.where(odd == 1, r - 2, r + 2)
        return copy(("far", e, j), rnear.at[e - 1, j], rfar.at[e - 1, j], (to, c))

    even = odd == 0
    takes_far = jnp.logical_or(
        jnp.logical_and(even, has_up), jnp.logical_and(jnp.logical_not(even), has_down)
    )
    gives_far = jnp.logical_or(
        jnp.logical_and(even, r < n_row - 2), jnp.logical_and(jnp.logical_not(even), r > 1)
    )

    def strip_low(e, part):
        top = margin if e == passes else 0
        if part == 0:
            return pl.multiple_of(jnp.where(even, tile, top), margin)
        return pl.multiple_of(jnp.where(even, top, tile), margin)

    def col_copy(e, side, part):
        if part == 1:
            low, size = strip, tile - strip
        elif e == 0:
            low, size = (0, tile)[part // 2], strip
        else:
            low, size = strip_low(e, part), margin if e == passes else strip
        rows = pl.ds(low, size)
        src = acc.at[2 * side, :, rows]
        dst = rcol.at[e, 1 - side, :, rows]
        return copy(("col", e, side, part), src, dst, (r, c - 1 if side == 0 else c + 1))

    def off_copy(side):
        return copy(("off", side), offs, roffs.at[1 - side], (r - 1 if side == 0 else r + 1, c))

    def start_cols(e, part):
        @pl.when(has_left)
        def _():
            col_copy(e, 0, part).start()

        @pl.when(has_right)
        def _():
            col_copy(e, 1, part).start()


    def piece_at(step, other_half, sign):
        place = 2 * lax.rem(z + (step if sign > 0 else nz - step), nz)
        return place + (1 - odd if other_half else odd)

    def own_or(g, held, step, other_half):
        if g == 0 and step == 0 and other_half == 0:
            return prb_ref
        return pf.at[g, held, piece_at(step, other_half, -1)]

    def ag_z(g, step):
        to = 2 * lax.rem(z + step, nz) + odd
        return copy(("agz", g, step), own_or(g, c, 0, 0), pf.at[g, c, r], (to, c))

    def ag_x(g, step):
        at = piece_at(step, 0, -1)
        return copy(("agx", g, step), own_or(g, c, step, 0), pf.at[g, c, at], (pair, c))

    def ag_sib(g, step, s):
        at = piece_at(step, s, -1)
        return copy(("ags", g, step, s), own_or(g, c, step, s), pf.at[g, c, at], (r, sibling))

    def ag_par(g, step, s, other):
        at = piece_at(step, s, -1)
        to = 2 * lax.rem(q + other, half) + core
        return copy(("agp", g, step, s, other), own_or(g, c, step, s), pf.at[g, c, at], (r, to))

    def ag_fwd(g, step, s, other):
        at = piece_at(step, s, -1)
        held = 2 * lax.rem(q + half - other, half) + core
        return copy(
            ("agf", g, step, s, other), pf.at[g, held, at], pf.at[g, held, at], (r, sibling)
        )

    def hand_on(g, step, s):
        for other in range(1, half):
            ag_par(g, step, s, other).start()
        ag_sib(g, step, s).start()

    def gather_send(g):
        for step in range(1, nz):
            ag_z(g, step).start()
        ag_x(g, 0).start()
        hand_on(g, 0, 0)

    def gather_first(g):
        for step in range(1, nz):
            ag_z(g, step).wait_recv()
            ag_x(g, step).start()
            hand_on(g, step, 0)

    def gather_second(g):
        for step in range(nz):
            ag_x(g, step).wait_recv()
            hand_on(g, step, 1)

    def gather_third(g):
        for s in range(2):
            for step in range(nz):
                for other in range(1, half):
                    ag_par(g, step, s, other).wait_recv()
                    ag_fwd(g, step, s, other).start()

    def gather_end(g):
        for s in range(2):
            for step in range(nz):
                ag_sib(g, step, s).wait_recv()
                for other in range(1, half):
                    ag_fwd(g, step, s, other).wait_recv()
        for step in range(nz):
            if step:
                ag_z(g, step).wait_send()
            ag_x(g, step).wait_send()
            for s in range(2):
                ag_sib(g, step, s).wait_send()
                for other in range(1, half):
                    ag_par(g, step, s, other).wait_send()
                    ag_fwd(g, step, s, other).wait_send()


    def rs_core(t, k, i):
        at = pl.ds(i * pieces, pieces)
        return copy(
            ("rsc", t, k, i), pg.at[2 * k + 1 - core, at], rc.at[t, k, at], (r, sibling)
        )

    def rs_par(t, step, s, other):
        at = piece_at(step, s, 1)
        to_q = lax.rem(q + other, half)
        return copy(
            ("rsp", t, step, s, other), hs.at[to_q, at], ry.at[t, other, at],
            (r, 2 * to_q + core),
        )

    def rs_x(t, step):
        return copy(("rsx", t, step), sx.at[step], rx.at[t, step], (pair, c))

    def rs_z(t, step):
        to = 2 * lax.rem(z + step, nz) + odd
        return copy(("rsz", t, step), ss.at[step], rr.at[t, step], (to, c))

    def sum_start(t, i):
        for k in range(half):
            rs_core(t, k, i).start()

    order = list(range(1, nz)) + [0]

    def sum_pass_on(t):
        for i in range(blocks):
            for k in range(half):
                rs_core(t, k, i).wait_recv()
        for s in (1, 0):
            for step in order:
                at = piece_at(step, s, 1)
                for other in range(1, half):
                    to_q = lax.rem(q + other, half)
                    hs[to_q, at] = pg[2 * to_q + core, at] + rc[t, to_q, at]
                    rs_par(t, step, s, other).start()

    def sum_piece(t, step, s):
        at = piece_at(step, s, 1)
        value = pg[c, at] + rc[t, q, at]
        for other in range(1, half):
            rs_par(t, step, s, other).wait_recv()
            value = value + ry[t, other, at]
        return value

    def sum_far(t):
        for step in order:
            sx[step] = sum_piece(t, step, 1)
            rs_x(t, step).start()

    def sum_near(t):
        for step in order:
            value = sum_piece(t, step, 0)
            rs_x(t, step).wait_recv()
            ss[step] = value + rx[t, step]
            if step:
                rs_z(t, step).start()

    def sum_end(t):
        value = ss[0]
        for step in range(1, nz):
            rs_z(t, step).wait_recv()
            value = value + rr[t, step]
        return value

    def sum_sent(t):
        for i in range(blocks):
            for k in range(half):
                rs_core(t, k, i).wait_send()
        for step in range(nz):
            for s in range(2):
                for other in range(1, half):
                    rs_par(t, step, s, other).wait_send()
            rs_x(t, step).wait_send()
            if step:
                rs_z(t, step).wait_send()


    for subset in range(SUBSETS):
        for d in range(2):
            offs[subset, d] = jnp.full(
                offs.shape[2:], pos_ref[order_ref[subset], d], jnp.int32
            )

    @pl.when(has_up)
    def _():
        row_copy(0, 0).start()
        off_copy(0).start()

    @pl.when(has_down)
    def _():
        row_copy(0, 1).start()
        off_copy(1).start()

    gather_send(0)
    loads[0].wait()

    def placed(values):
        rows = values.shape[0]
        spot = lax.broadcasted_iota(jnp.int32, (rows, LANES), 1) >= margin
        first = pltpu.roll(values[:, :LANES], margin, 1)
        second = pltpu.roll(values[:, LANES:], margin, 1)
        zero = jnp.zeros_like(first)
        return (
            jnp.where(spot, first, zero), jnp.where(spot, second, first),
            jnp.where(spot, zero, second),
        )

    for plane in range(2):
        for k in range(2):
            gpad[plane, k, 0:strip] = jnp.zeros((strip, LANES), f32)
            gpad[plane, k, strip + width :] = jnp.zeros((strip, LANES), f32)
        for low in range(0, tile, margin):
            parts = placed(obj_ref[plane, low : low + margin])
            for b in range(3):
                acc[b, plane, margin + low : 2 * margin + low] = parts[b]
    start_cols(0, 1)
    gather_first(0)

    def halo_rows(side, at):
        for plane in range(2):
            parts = placed(rrow[side, plane])
            for b in range(3):
                acc[b, plane, at : at + margin] = parts[b]

    def halo_zero(at):
        for plane in range(2):
            for b in range(3):
                acc[b, plane, at : at + margin] = jnp.zeros((margin, LANES), f32)

    @pl.when(has_down)
    def _():
        row_copy(0, 0).wait_recv()
        off_copy(0).wait_recv()
        halo_rows(1, tile + margin)

    @pl.when(jnp.logical_not(has_down))
    def _():
        halo_zero(tile + margin)

    start_cols(0, 2)
    gather_second(0)

    @pl.when(has_up)
    def _():
        row_copy(0, 1).wait_recv()
        off_copy(1).wait_recv()
        halo_rows(0, 0)

    @pl.when(jnp.logical_not(has_up))
    def _():
        halo_zero(0)

    start_cols(0, 0)
    gather_third(0)

    def take_cols(e):
        for part in range(3):
            @pl.when(has_left)
            def _():
                col_copy(e, 1, part).wait_recv()

            @pl.when(has_right)
            def _():
                col_copy(e, 0, part).wait_recv()

    def sent(e):
        if e == 0:
            @pl.when(has_up)
            def _():
                row_copy(e, 0).wait_send()

            @pl.when(has_down)
            def _():
                row_copy(e, 1).wait_send()
        else:
            for j in range(chunks(e)):
                near_copy(e, j).wait_send()

            @pl.when(gives_far)
            def _():
                for j in range(chunks(e)):
                    far_copy(e, j).wait_send()

        for part in range(3):
            @pl.when(has_left)
            def _():
                col_copy(e, 0, part).wait_send()

            @pl.when(has_right)
            def _():
                col_copy(e, 1, part).wait_send()

    for side, there in ((0, has_left), (1, has_right)):
        @pl.when(jnp.logical_not(there))
        def _():
            for e in range(passes + 1):
                rcol[e, side] = jnp.zeros(rcol.shape[2:], f32)

    take_cols(0)
    for plane in range(2):
        ext[0, plane] = acc[0, plane] + rcol[0, 0, plane]
        ext[1, plane] = acc[1, plane]
        ext[2, plane] = acc[2, plane] + rcol[0, 1, plane]
    sent(0)

    @pl.when(has_up)
    def _():
        off_copy(0).wait_send()

    @pl.when(has_down)
    def _():
        off_copy(1).wait_send()

    gather_end(0)
    for load in loads[1:]:
        load.wait()

    def probe_block(g, m, i):
        parts = [
            pf[g, k, pl.ds(i * pieces, pieces), m].reshape(block, pw) for k in range(n_col)
        ]
        return (
            jnp.concatenate(parts[:half], 1), jnp.concatenate(parts[half:], 1)
        )

    def gradient_rows(plane, low, size):
        return jnp.concatenate([gpad[plane, k, pl.ds(low, size), :] for k in range(2)], 1)

    def unpacked(mask, values):
        zero = jnp.zeros_like(values[:, :LANES])
        return (
            jnp.where(mask, values[:, :LANES], zero), values[:, LANES:],
            jnp.where(mask, zero, values[:, :LANES]),
        )

    row_low = jnp.where(has_up, 0, margin)
    row_high = jnp.where(has_down, extent, extent - margin)
    col_low = jnp.where(has_left, 0, margin)
    col_high = jnp.where(has_right, LANES, margin)

    for number in range(passes):
        outer_step, subset = number // SUBSETS, number % SUBSETS
        g = outer_step
        e = number + 1
        last = e == passes
        chosen = order_ref[subset]
        a = pos_ref[chosen, 0]
        b = pos_ref[chosen, 1]
        back = lax.rem(LANES - b, LANES)
        ahead = lax.rem(b, LANES)

        @pl.loop(0, blocks)
        def _(i):
            rows = pl.ds(pl.multiple_of(i * block, block), block)
            planes = []
            for plane in range(2):
                turned = [
                    pltpu.roll(ext[k, plane, pl.ds(a + i * block, block), :], back, 1)
                    for k in range(3)
                ]
                inside = lanes < LANES - b
                window = jnp.concatenate(
                    [jnp.where(inside, turned[k], turned[k + 1]) for k in range(2)], 1
                )
                win[plane, rows] = window
                planes.append(window)
            for m in range(modes):
                p_re, p_im = probe_block(g, m, i)
                wave = jnp.concatenate(
                    [p_re * planes[0] - p_im * planes[1], p_re * planes[1] + p_im * planes[0]], 1
                )
                ew[m, rows] = wave
                xb[m, rows] = wave.astype(jnp.bfloat16)

        def transform(source, m, rows, direction, table_ref):
            cos = jnp.dot(lt_ref[0, rows], source[m], preferred_element_type=f32)
            sin = jnp.dot(lt_ref[1, rows], source[m], preferred_element_type=f32)
            mixed = jnp.concatenate(
                [
                    cos[:, :width] + direction * sin[:, width:],
                    cos[:, width:] - direction * sin[:, :width],
                ],
                1,
            ).astype(jnp.bfloat16)
            return jnp.dot(mixed, table_ref[...], preferred_element_type=f32)

        @pl.loop(0, blocks)
        def _(i):
            rows = pl.ds(pl.multiple_of(i * block, block), block)
            far = [transform(xb, m, rows, 1.0, rf_ref) for m in range(modes)]
            intensity = sum(
                f[:, :width] * f[:, :width] + f[:, width:] * f[:, width:] for f in far
            )
            scaling = meas_ref[chosen, rows] * jnp.minimum(
                lax.rsqrt(intensity), 1.0 / amp_floor
            )
            scaling = jnp.concatenate([scaling, scaling], 1)
            for m in range(modes):
                zb[m, rows] = (far[m] * scaling).astype(jnp.bfloat16)

        mask = lanes >= b
        for i in range(blocks):
            rows = slice(i * block, (i + 1) * block)
            w_re, w_im = win[0, rows], win[1, rows]
            g_re = g_im = None
            for m in range(modes):
                change = transform(zb, m, rows, -1.0, ri_ref) - ew[m, rows]
                c_re, c_im = change[:, :width], change[:, width:]
                p_re, p_im = probe_block(g, m, i)
                part_re, part_im = p_re * c_re + p_im * c_im, p_re * c_im - p_im * c_re
                g_re = part_re if m == 0 else g_re + part_re
                g_im = part_im if m == 0 else g_im + part_im
                grad = jnp.concatenate(
                    [w_re * c_re + w_im * c_im, w_re * c_im - w_im * c_re], 1
                )
                at = slice(i * pieces, (i + 1) * pieces)
                for k in range(n_col):
                    value = grad[:, k * pw : (k + 1) * pw].reshape(pieces, pr, pw)
                    if subset:
                        value = value + pg[k, at, m]
                    pg[k, at, m] = value
            for plane, values in enumerate((g_re, g_im)):
                first = pltpu.roll(values[:, :LANES], ahead, 1)
                second = pltpu.roll(values[:, LANES:], ahead, 1)
                at = slice(strip + i * block, strip + (i + 1) * block)
                gpad[plane, 0, at] = jnp.where(mask, first, second)
                gpad[plane, 1, at] = jnp.where(mask, second, first)
            if subset == SUBSETS - 1:
                sum_start(outer_step, i)

        for j in range(chunks(e)):
            if last:
                plane, top, bottom = j, 0, extent - margin
            else:
                plane, top = j // 2, j % 2 * margin
                bottom = tile + top
            srow[j] = gradient_rows(plane, strip + top - a, margin) + gradient_rows(
                plane, strip + bottom - a, margin
            )
            near_copy(e, j).start()

        if subset == SUBSETS - 1:
            sum_pass_on(outer_step)

        for low in (strip, 0, tile):
            for plane in range(2):
                parts = unpacked(mask, gradient_rows(plane, strip + low - a, strip))
                for k in range(3):
                    acc[k, plane, low : low + strip] = parts[k]
            if low == strip:
                start_cols(e, 1)

        def add_rows(part, take, arrived):
            from_down = even if part == 0 else jnp.logical_not(even)
            side = jnp.where(from_down, 1, 0)
            low = strip_low(e, part)
            there_a, there_b = roffs[side, subset, 0, 0:1, :], roffs[side, subset, 1, 0:1, :]
            spot = lax.broadcasted_iota(jnp.int32, (margin, LANES), 1) >= there_b
            row_at = lax.broadcasted_iota(jnp.int32, (margin, LANES), 0)
            for j in range(chunks(e)):
                take(e, j).wait_recv()
                if part == 0:
                    @pl.when(gives_far)
                    def _():
                        far_copy(e, j).start()

                plane, top = (j, 0) if last else (j // 2, j % 2 * margin)
                under = row_at + (margin if last else top)
                kept = jnp.where(from_down, row_at + top - there_a, there_a - 1 - under) >= 0
                values = arrived[e - 1, j]
                values = jnp.where(
                    jnp.concatenate([kept, kept], 1), values, jnp.zeros_like(values)
                )
                parts = unpacked(spot, values)
                rows = pl.ds(pl.multiple_of(low + top, margin), margin)
                for k in range(3):
                    acc[k, plane, rows] += parts[k]

        if subset == SUBSETS - 1:
            sum_far(outer_step)
        add_rows(0, near_copy, rnear)
        start_cols(e, 0)
        if subset == SUBSETS - 1:
            sum_near(outer_step)

        @pl.when(takes_far)
        def _():
            add_rows(2, far_copy, rfar)

        start_cols(e, 2)

        if subset == SUBSETS - 1:
            total = sum_end(outer_step)
            piece = pf[g, c, r] + probe_rate * total
            if last:
                out_prb[...] = piece
            else:
                pf[g + 1, c, r] = piece
                gather_send(g + 1)
                gather_first(g + 1)
                gather_second(g + 1)
                gather_third(g + 1)

        take_cols(e)
        if not last:
            for low in range(0, extent, block):
                row_at = lax.broadcasted_iota(jnp.int32, (block, LANES), 0) + low
                good = jnp.logical_and(row_at >= row_low, row_at < row_high)
                rows = slice(low, low + block)
                for plane in range(2):
                    for k in range(3):
                        value = acc[k, plane, rows]
                        kept = good
                        if k == 0:
                            value = value + rcol[e, 0, plane, rows]
                            kept = jnp.logical_and(good, lanes >= col_low)
                        elif k == 2:
                            value = value + rcol[e, 1, plane, rows]
                            kept = jnp.logical_and(good, lanes < col_high)
                        ext[k, plane, rows] += jnp.where(
                            kept, object_rate * value, jnp.zeros_like(value)
                        )
        else:
            spot = lax.broadcasted_iota(jnp.int32, (margin, LANES), 1) < margin
            for low in range(0, tile, margin):
                rows = slice(margin + low, 2 * margin + low)
                for plane in range(2):
                    turned = []
                    for k in range(3):
                        value = acc[k, plane, rows]
                        if k != 1:
                            value = value + rcol[e, k // 2, plane, rows]
                        value = ext[k, plane, rows] + object_rate * value
                        turned.append(pltpu.roll(value, margin, 1))
                    out_obj[plane, low : low + margin] = jnp.concatenate(
                        [jnp.where(spot, turned[k], turned[k + 1]) for k in range(2)], 1
                    )
        sent(e)
        if subset == SUBSETS - 1:
            sum_sent(outer_step)
            if not last:
                gather_end(g + 1)


def tiles(object_field, probe_modes, measured, positions, subset_order):
    n_row, n_col = lax.axis_size("row"), lax.axis_size("col")
    tile = object_field.shape[1]
    modes, pr, pw = probe_modes.shape
    pos_count, width = measured.shape[2], measured.shape[3]
    strip = 2 * MARGIN
    fits = (
        pos_count == SUBSETS and strip == LANES and width == 2 * LANES and tile == width
        and n_col % 2 == 0 and pw == LANES and pr % 8 == 0 and strip % pr == 0
        and n_row % 2 == 0
    )
    if not fits:
        return shards(object_field, probe_modes, measured, positions, subset_order)
    extent = tile + strip
    passes = OUTER * SUBSETS
    half = n_col // 2
    probe_rate = 0.5 / (pos_count * n_row * n_col)
    left_tables, right_forward, right_inverse = host_tables(width)
    f32, bf16 = jnp.float32, jnp.bfloat16
    vmem = pl.BlockSpec(memory_space=pltpu.VMEM)
    smem = pl.BlockSpec(memory_space=pltpu.SMEM)
    copies = (passes + 1) * 16 + 4 + 4 * OUTER * n_row * n_col
    far = pl.BlockSpec(memory_space=pltpu.HBM)
    return pl.pallas_call(
        functools.partial(kernel, n_row, n_col, probe_rate),
        out_shape=(
            jax.ShapeDtypeStruct(object_field.shape, f32),
            jax.ShapeDtypeStruct(probe_modes.shape, f32),
        ),
        in_specs=[smem, smem] + [far] * 6,
        out_specs=(vmem, vmem),
        scratch_shapes=[
            pltpu.VMEM((3, 2, extent, LANES), f32),
            pltpu.VMEM((3, 2, extent, LANES), f32),
            pltpu.VMEM((2, 2, width + 2 * strip, LANES), f32),
            pltpu.VMEM((2, width, width), f32),
            pltpu.VMEM((modes, width, 2 * width), f32),
            pltpu.VMEM((modes, width, 2 * width), bf16),
            pltpu.VMEM((modes, width, 2 * width), bf16),
            pltpu.VMEM((SUBSETS, 2, 8, LANES), jnp.int32),
            pltpu.VMEM((2, SUBSETS, 2, 8, LANES), jnp.int32),
            pltpu.VMEM((4, MARGIN, width), f32),
            pltpu.VMEM((2, 2, MARGIN, width), f32),
            pltpu.VMEM((passes, 4, MARGIN, width), f32),
            pltpu.VMEM((passes, 4, MARGIN, width), f32),
            pltpu.VMEM((passes + 1, 2, 2, extent, LANES), f32),
            pltpu.VMEM((OUTER, n_col, n_row, modes, pr, pw), f32),
            pltpu.VMEM((n_col, n_row, modes, pr, pw), f32),
            pltpu.VMEM((half, n_row, modes, pr, pw), f32),
            pltpu.VMEM((OUTER, half, n_row, modes, pr, pw), f32),
            pltpu.VMEM((OUTER, half, n_row, modes, pr, pw), f32),
            pltpu.VMEM((n_row // 2, modes, pr, pw), f32),
            pltpu.VMEM((OUTER, n_row // 2, modes, pr, pw), f32),
            pltpu.VMEM((n_row // 2, modes, pr, pw), f32),
            pltpu.VMEM((OUTER, n_row // 2, modes, pr, pw), f32),
            pltpu.VMEM(object_field.shape, f32),
            pltpu.VMEM((pos_count, width, width), f32),
            pltpu.VMEM(left_tables.shape, bf16),
            pltpu.VMEM(right_forward.shape, bf16),
            pltpu.VMEM(right_inverse.shape, bf16),
            pltpu.SemaphoreType.DMA((copies,)),
            pltpu.SemaphoreType.DMA((copies,)),
            pltpu.SemaphoreType.DMA((6,)),
        ],
        compiler_params=pltpu.CompilerParams(
            collective_id=0, has_side_effects=True, vmem_limit_bytes=63 * 1024 * 1024 + 512 * 1024
        ),
    )(
        positions[0, 0], subset_order[0, 0], object_field, probe_modes, measured[0, 0],
        jnp.asarray(left_tables), jnp.asarray(right_forward), jnp.asarray(right_inverse),
    )


def solution(mesh):
    in_specs = (
        P(None, "row", "col"),
        P(None, "row", "col"),
        P("row", "col", None, None, None),
        P("row", "col", None, None),
        P("row", "col", None),
    )
    out_specs = (P(None, "row", "col"), P(None, "row", "col"))
    return jax.shard_map(tiles, mesh=mesh, in_specs=in_specs, out_specs=out_specs, check_vma=False)
```
